32 devices in a mesh: rep: 16 (over z, y, x), tp: 2 (over core).
Axes of the slice: x: 2, y: 2, z: 4, core: 2. Of those that a mesh axis runs over, the one named last changes fastest.
Arguments:
- kv_pool: bfloat16 [256, 128, 1024], P('rep', None, 'tp'), may hold values from -6 to 6
- page_table: int32 [64, 4], P('rep'), may hold values from 0 to 15, as said below
- req_lengths: int32 [64], P('rep'), may hold values from 1 to 511, as said below
- leave_slot: int32 [16], P('rep'), may hold values from 0 to 3
- target_rep: int32 [16], P('rep'), may hold values from 0 to 15, as said below
- qkv_new: bfloat16 [64, 2560], P('rep', 'tp'), may hold values from -8.2 to 8.2
- residual_in: bfloat16 [64, 1536], P('rep'), may hold values from -6 to 6
- expert_ids: int32 [64, 1], P('rep'), may hold values from 0 to 1
- gate_weights: bfloat16 [64, 1], P('rep'), may hold values from 0.099609375 to 0.69921875
- norm_gain: float32 [1536], replicated, may hold values from 0.1 to 1.9
- out_proj: bfloat16 [1536, 1536], P('tp'), may hold values from -0.15625 to 0.15625
- expert_in: bfloat16 [2, 1536, 512], P('tp'), may hold values from -0.15625 to 0.15625
- expert_down: bfloat16 [2, 256, 1536], P('tp'), may hold values from -0.375 to 0.375
Outputs:
- hidden_out: bfloat16 [64, 1536], P('rep', 'tp')
- new_pages: bfloat16 [64, 128, 1024], P('rep', None, 'tp')
- arrived: bfloat16 [64, 128, 1024], P('rep', None, 'tp')
The draws below stay inside these ranges and needn't reach their ends.
Inputs may be any that keep to these rules, and one draw needn't show every extreme that they name: `req_lengths`: in every draw the request that leaves some replica has length 511. `page_table`: the 4 rows of one replica hold each of its 16 pool pages once. `target_rep`: the targets form one cycle through all replicas: every replica receives exactly one request and none keeps its own; in every draw some replica sends to the replica half the axis of replicas away.
All inputs are finite; a program needn't handle non-finite values.
Results may differ from the reference program's by a relative error of at most 0.005.
Values may be sent and summed in bfloat16 or wider, within the bound.
No kernel may reach another device: no remote copies, remote signals or barrier semaphores. Data moves between devices by JAX's collectives and lax.ppermute only.
A program may use at most 64 MiB of HBM per device.

```python
import math
import jax
import jax.numpy as jnp
from jax import lax

D = 1536
QH = 24
KVH = 8
HD = 64
FF = 256
PAGE = 128
MAXP = 4
REQ = 4
EXPERTS = 2
TOP = 1
POOL = 16
REQS = 64
N_REP = 16


def leave_slots(key):
    return jax.random.randint(jax.random.fold_in(key, 11), (N_REP,), 0, REQ, dtype=jnp.int32)


def draw_leave_slot(key, part):
    return leave_slots(key)


def draw_target_rep(key, part):
    scores = jax.random.permutation(jax.random.fold_in(key, 13), N_REP).astype(jnp.int32)
    first = jax.random.randint(jax.random.fold_in(key, 14), (), 0, N_REP, dtype=jnp.int32)
    second = (first + N_REP // 2) % N_REP
    scores = scores.at[first].set(-2).at[second].set(-1)
    order = jnp.argsort(scores, stable=True).astype(jnp.int32)
    return jnp.zeros((N_REP,), jnp.int32).at[order].set(jnp.roll(order, -1))


def draw_req_lengths(key, part):
    limit = MAXP * PAGE
    first = jax.random.randint(jax.random.fold_in(key, 21), (REQS,), 0, limit, dtype=jnp.int32)
    second = jax.random.randint(jax.random.fold_in(key, 22), (REQS,), 0, limit, dtype=jnp.int32)
    drawn = 1 + first * second // limit
    chosen_rep = jax.random.randint(jax.random.fold_in(key, 23), (), 0, N_REP, dtype=jnp.int32)
    longest = chosen_rep * REQ + leave_slots(key)[chosen_rep]
    return drawn.at[longest].set(limit - 1)


def draw_page_table(key, part):
    table_key = jax.random.fold_in(key, 31)

    def one_replica(index):
        return jax.random.permutation(jax.random.fold_in(table_key, index), POOL)
    tables = jax.vmap(one_replica)(jnp.arange(N_REP, dtype=jnp.int32))
    return tables.reshape(REQS, MAXP).astype(jnp.int32)


def draw_kv_pool(key, part):
    full_shape = (N_REP * POOL, PAGE, KVH, 2, HD)
    drawn = jnp.clip(jax.random.normal(jax.random.fold_in(key, 42), full_shape, jnp.float32), -6.0, 6.0)
    return drawn.reshape(N_REP * POOL, PAGE, KVH * 2 * HD).astype(jnp.bfloat16)


def draw_qkv_new(key, part):
    group = QH // KVH
    full_shape = (REQS, KVH, group + 2, HD)
    drawn = jnp.clip(jax.random.normal(jax.random.fold_in(key, 51), full_shape, jnp.float32), -6.0, 6.0)
    return drawn.reshape(REQS, KVH * (group + 2) * HD).astype(jnp.bfloat16)


def level_of(key, extent, pieces, low, high):
    factor_of = 1.0
    for dim, shards_of in pieces:
        steps = jax.random.uniform(jax.random.fold_in(jax.random.fold_in(key, 6), dim), (shards_of,), jnp.float32, low / len(pieces), high / len(pieces))
        factor_of = factor_of * jnp.repeat(jnp.exp(steps), extent[dim] // shards_of).reshape((-1,) + (1,) * (len(extent) - 1 - dim))
    return factor_of


def choose_distinct(key, rows, count, top, lift):
    ranking = jax.random.permutation(jax.random.fold_in(key, 1), count)
    pull = ranking
    for power in range(3):
        pull = pull * pull // count
    pull = pull * lift // count
    tickets = jax.random.randint(jax.random.fold_in(key, 2), (rows, count), 0, 4096) + pull
    sure = jax.random.permutation(jax.random.fold_in(key, 3), rows)[jnp.arange(count) % rows]
    tickets = jnp.where(jnp.arange(rows)[:, None] == sure[None, :], 1 << 14, tickets)
    priority = tickets * count + jnp.arange(count)
    return lax.top_k(priority.astype(jnp.int32), top)[1].astype(jnp.int32)


def normal_values(rng, shape, spread, most, split=(), held_as=jnp.bfloat16):
    entries = spread * jax.random.normal(rng, shape, jnp.float32)
    if split:
        entries = entries * level_of(rng, shape, split, -0.22, 0.18)
    return jnp.clip(entries, -most, most).astype(held_as)


def setup_inputs(seed: int = 0) -> dict:
    key_of = jax.random.split(jax.random.key(seed), 14)
    kv_pool = draw_kv_pool(jax.random.fold_in(key_of[13], 71), 0)
    page_table = draw_page_table(jax.random.fold_in(key_of[13], 71), 0)
    req_lengths = draw_req_lengths(jax.random.fold_in(key_of[13], 71), 0)
    leave_slot = draw_leave_slot(jax.random.fold_in(key_of[13], 71), 0)
    target_rep = draw_target_rep(jax.random.fold_in(key_of[13], 71), 0)
    qkv_new = draw_qkv_new(jax.random.fold_in(key_of[13], 71), 0)
    residual_in = normal_values(key_of[6], (REQS, D), 1.0, 6.0, ((0, 16),))
    expert_ids = choose_distinct(key_of[7], REQS, EXPERTS, TOP, 4096)
    gate_weights = jnp.clip(0.099609375 + 0.5996094 * jax.random.uniform(key_of[8], (REQS, TOP), jnp.float32) ** level_of(key_of[8], (REQS, TOP), ((0, 16),), -0.2, 0.2), 0.099609375, 0.69921875).astype(jnp.bfloat16)
    norm_gain = jnp.clip(1.0 + 0.18 * jax.random.normal(key_of[9], (D,), jnp.float32), 0.1, 1.9)
    out_proj = normal_values(key_of[10], (QH * HD, D), (QH * HD) ** -0.5, 0.15625, ((0, 2),))
    expert_in = normal_values(key_of[11], (EXPERTS, D, 2 * FF), D ** -0.5, 0.15625, ((0, 2),))
    expert_down = normal_values(key_of[12], (EXPERTS, FF, D), FF ** -0.5, 0.375, ((0, 2),))
    return dict(kv_pool=kv_pool, page_table=page_table, req_lengths=req_lengths, leave_slot=leave_slot, target_rep=target_rep, qkv_new=qkv_new, residual_in=residual_in, expert_ids=expert_ids, gate_weights=gate_weights, norm_gain=norm_gain, out_proj=out_proj, expert_in=expert_in, expert_down=expert_down)


def reference(kv_pool, page_table, req_lengths, leave_slot, target_rep, qkv_new, residual_in, expert_ids, gate_weights, norm_gain, out_proj, expert_in, expert_down):
    group = QH // KVH
    col_total = 2 * KVH * HD
    replicas = jnp.arange(N_REP, dtype=jnp.int32)
    source_rep = jnp.zeros((N_REP,), jnp.int32).at[target_rep].set(replicas)
    global_slot = replicas * REQ + leave_slot
    anchor = jnp.arange(REQS, dtype=jnp.int32).at[global_slot].set(source_rep * REQ + leave_slot[source_rep])
    qkv_now = qkv_new[anchor]
    resid_now = residual_in[anchor]
    len_now = req_lengths[anchor]
    ids_now = expert_ids[anchor]
    gates_now = gate_weights[anchor]
    page_rows = (anchor // REQ * POOL)[:, None] + page_table[anchor]

    def per_replica(index):
        start_row = (index * REQ).astype(jnp.int32)
        rows_here = lax.dynamic_slice_in_dim(page_rows, start_row, REQ, 0)
        cache_rows = kv_pool[rows_here].reshape(REQ, MAXP * PAGE, col_total)
        qkv_here = lax.dynamic_slice_in_dim(qkv_now, start_row, REQ, 0).reshape(REQ, KVH, group + 2, HD)
        len_here = lax.dynamic_slice_in_dim(len_now, start_row, REQ, 0)
        fresh = qkv_here[:, :, group:, :].reshape(REQ, col_total)
        positions = jnp.arange(MAXP * PAGE, dtype=jnp.int32)
        at_token = positions[None, :] == len_here[:, None]
        cache_rows = jnp.where(at_token[:, :, None], fresh[:, None, :], cache_rows)
        split_cache = cache_rows.reshape(REQ, MAXP * PAGE, KVH, 2, HD).astype(jnp.float32)
        queries = qkv_here[:, :, :group, :].astype(jnp.float32)
        scores = jnp.einsum('rhgd,rlhd->rhgl', queries, split_cache[:, :, :, 0, :]) * (1.0 / math.sqrt(HD))
        visible = positions[None, :] <= len_here[:, None]
        scores = jnp.where(visible[:, None, None, :], scores, -jnp.inf)
        top_score = lax.optimization_barrier(jnp.max(scores, axis=-1, keepdims=True))
        weights = jnp.exp(scores - top_score)
        probs = (weights / lax.optimization_barrier(jnp.sum(weights, axis=-1, keepdims=True))).astype(jnp.bfloat16)
        attn_here = jnp.einsum('rhgl,rlhd->rhgd', probs.astype(jnp.float32), split_cache[:, :, :, 1, :])
        attn_here = attn_here.astype(jnp.bfloat16).reshape(REQ, QH * HD)
        paged = cache_rows.reshape(REQ, MAXP, PAGE, col_total)
        page_pick = jnp.take_along_axis(paged, (len_here // PAGE)[:, None, None, None], axis=1)[:, 0]
        came_in = lax.dynamic_index_in_dim(paged, leave_slot[index], 0, keepdims=False)
        return (attn_here, page_pick, came_in)
    attn_all, pages_all, came_all = lax.map(per_replica, replicas)
    attn_out = attn_all.reshape(REQS, QH * HD)
    new_pages = pages_all.reshape(REQS, PAGE, col_total)
    arrived = came_all.reshape(N_REP * MAXP, PAGE, col_total)
    stream = resid_now.astype(jnp.float32) + jnp.dot(attn_out, out_proj, preferred_element_type=jnp.float32)
    mean_sq = lax.optimization_barrier(jnp.mean(stream * stream, axis=1, keepdims=True))
    normed = (stream * lax.rsqrt(mean_sq + 1e-05) * norm_gain).astype(jnp.bfloat16)
    expert_mix = jnp.zeros((REQS, D), jnp.float32)
    for expert in range(EXPERTS):
        route_share = lax.optimization_barrier(jnp.sum(jnp.where(ids_now == expert, gates_now.astype(jnp.float32), 0.0), axis=1))
        up_both = jnp.dot(normed, expert_in[expert], preferred_element_type=jnp.float32)
        acted = (jax.nn.silu(up_both[:, :FF]) * up_both[:, FF:]).astype(jnp.bfloat16)
        expert_mix = expert_mix + route_share[:, None] * jnp.dot(acted, expert_down[expert], preferred_element_type=jnp.float32)
    hidden_out = (stream + expert_mix).astype(jnp.bfloat16)
    return (hidden_out, new_pages, arrived)
```

```python
import math

import jax
import jax.numpy as jnp
from jax import lax
from jax.experimental import pallas as pl
from jax.experimental.pallas import tpu as pltpu
from jax.sharding import PartitionSpec as P

QH = 24
KVH = 8
HD = 64
FF = 256
PAGE = 128
MAXP = 4
GROUP = QH // KVH
SPAN = MAXP * PAGE
LANES = 128
EXTRA = 8
VMEM_BYTES = 32 * 1024 * 1024

SMEM = pl.BlockSpec(memory_space=pltpu.SMEM)
VMEM = pl.BlockSpec(memory_space=pltpu.VMEM)
ANY = pl.BlockSpec(memory_space=pl.ANY)


def row_of(values, index):
    at_row = lax.broadcasted_iota(jnp.int32, values.shape, 0) == index
    return jnp.sum(jnp.where(at_row, values, 0.0), axis=0, keepdims=True)


def put_row(ref, lead, row, fresh):
    start = pl.multiple_of(row // 16 * 16, 16)
    block = ref[lead, pl.ds(start, 16), :].astype(jnp.float32)
    at_row = lax.broadcasted_iota(jnp.int32, block.shape, 0) == row - start
    ref[lead, pl.ds(start, 16), :] = jnp.where(at_row, fresh, block).astype(ref.dtype)


def pack_kernel(leave_ref, target_ref, table_ref, lens_ref, qkv_ref, pool_ref, send_ref, pages, sems):
    leave = leave_ref[0]
    copies = [
        pltpu.make_async_copy(pool_ref.at[table_ref[leave, p]], pages.at[p], sems.at[p])
        for p in range(MAXP)
    ]
    for copy in copies:
        copy.start()
    pieces, _, _ = send_ref.shape
    cols = pages.shape[2]
    rows = SPAN // pieces
    body = cols // LANES * rows
    ticket = jnp.full((pieces, EXTRA, LANES), target_ref[0].astype(jnp.float32), jnp.float32)
    send_ref[:, body:, :] = ticket.astype(send_ref.dtype)
    qkv = row_of(qkv_ref[...].astype(jnp.float32), leave)
    width = (GROUP + 2) * HD
    fresh = jnp.concatenate(
        [qkv[:, h * width + GROUP * HD : (h + 1) * width] for h in range(cols // LANES)], axis=1
    )
    for copy in copies:
        copy.wait()
    length = lens_ref[leave]
    put_row(pages, length // PAGE, length % PAGE, fresh)
    for j in range(pieces):
        page, start = j * rows // PAGE, j * rows % PAGE
        for c in range(cols // LANES):
            send_ref[j, c * rows : (c + 1) * rows, :] = pages[
                page, start : start + rows, c * LANES : (c + 1) * LANES
            ]


def pack(leave_slot, target_rep, page_table, req_lengths, qkv_new, kv_pool, pieces):
    cols = kv_pool.shape[2]
    slot_rows = SPAN // pieces * (cols // LANES) + EXTRA
    return pl.pallas_call(
        pack_kernel,
        out_shape=jax.ShapeDtypeStruct((pieces, slot_rows, LANES), kv_pool.dtype),
        in_specs=[SMEM, SMEM, SMEM, SMEM, VMEM, ANY],
        out_specs=VMEM,
        scratch_shapes=[
            pltpu.VMEM((MAXP, PAGE, cols), kv_pool.dtype),
            pltpu.SemaphoreType.DMA((MAXP,)),
        ],
        compiler_params=pltpu.CompilerParams(vmem_limit_bytes=VMEM_BYTES),
        name="pack",
    )(leave_slot, target_rep, page_table, req_lengths, qkv_new, kv_pool)


def attend_kernel(
    table_ref, lens_ref, query_ref, fresh_ref, pool_ref, proj_ref, head_ref, new_ref,
    cache, proj, rows, page_sems, proj_sem, new_sems,
):
    num_req, heads, cols = query_ref.shape
    used = cols // LANES * GROUP
    reads = [
        [
            pltpu.make_async_copy(
                pool_ref.at[table_ref[r, p]], cache.at[r, pl.ds(p * PAGE, PAGE)], page_sems.at[r, p]
            )
            for p in range(MAXP)
        ]
        for r in range(num_req)
    ]
    for request in reads:
        for copy in request:
            copy.start()
    proj_read = pltpu.make_async_copy(proj_ref, proj, proj_sem)
    proj_read.start()
    fresh = fresh_ref[...].astype(jnp.float32)
    writes = []
    for r in range(num_req):
        for copy in reads[r]:
            copy.wait()
        length = lens_ref[r]
        put_row(cache, r, length, fresh[r : r + 1, :])
        start = pl.multiple_of(length // PAGE * PAGE, PAGE)
        write = pltpu.make_async_copy(cache.at[r, pl.ds(start, PAGE)], new_ref.at[r], new_sems.at[r])
        write.start()
        writes.append(write)
        held = cache[r]
        scores = lax.dot_general(
            query_ref[r], held, (((1,), (1,)), ((), ())), preferred_element_type=jnp.float32
        ) * (1.0 / math.sqrt(HD))
        positions = lax.broadcasted_iota(jnp.int32, scores.shape, 1)
        scores = jnp.where(positions <= length, scores, -jnp.inf)
        weights = jnp.exp(scores - jnp.max(scores, axis=1, keepdims=True))
        probs = (weights / jnp.sum(weights, axis=1, keepdims=True)).astype(held.dtype)
        rows[r] = jnp.dot(probs, held, preferred_element_type=jnp.float32)
    attn = jnp.concatenate(
        [
            jnp.concatenate(
                [
                    rows[r, i : i + 1, i // GROUP * LANES + HD : (i // GROUP + 1) * LANES]
                    for i in range(used)
                ],
                axis=1,
            )
            for r in range(num_req)
        ],
        axis=0,
    ).astype(proj.dtype)
    proj_read.wait()
    head_ref[...] = jnp.dot(attn, proj[...], preferred_element_type=jnp.float32)
    for write in writes:
        write.wait()


def attend(page_table, req_lengths, qkv_new, kv_pool, out_proj):
    num_req = qkv_new.shape[0]
    cols = kv_pool.shape[2]
    head_local = cols // LANES
    split = qkv_new.reshape(num_req, head_local, GROUP + 2, HD)
    fresh = split[:, :, GROUP:, :].reshape(num_req, cols)
    own_head = jnp.arange(head_local)[:, None] == jnp.arange(head_local)[None, :]
    queries = jnp.where(
        own_head[None, :, None, :, None], split[:, :, :GROUP, None, :], jnp.zeros((), qkv_new.dtype)
    )
    queries = jnp.pad(queries, ((0, 0), (0, 0), (0, 0), (0, 0), (0, HD)))
    queries = queries.reshape(num_req, head_local * GROUP, cols)
    heads = -(-head_local * GROUP // 16) * 16
    queries = jnp.pad(queries, ((0, 0), (0, heads - head_local * GROUP), (0, 0)))
    width = out_proj.shape[1]
    return pl.pallas_call(
        attend_kernel,
        out_shape=(
            jax.ShapeDtypeStruct((num_req, width), jnp.float32),
            jax.ShapeDtypeStruct((num_req, PAGE, cols), kv_pool.dtype),
        ),
        in_specs=[SMEM, SMEM, VMEM, VMEM, ANY, ANY],
        out_specs=(VMEM, ANY),
        scratch_shapes=[
            pltpu.VMEM((num_req, SPAN, cols), kv_pool.dtype),
            pltpu.VMEM(out_proj.shape, out_proj.dtype),
            pltpu.VMEM((num_req, heads, cols), jnp.float32),
            pltpu.SemaphoreType.DMA((num_req, MAXP)),
            pltpu.SemaphoreType.DMA,
            pltpu.SemaphoreType.DMA((num_req,)),
        ],
        compiler_params=pltpu.CompilerParams(vmem_limit_bytes=VMEM_BYTES),
        cost_estimate=pl.CostEstimate(
            flops=2 * num_req * (2 * heads * SPAN * cols + out_proj.size),
            bytes_accessed=2 * (num_req * SPAN * cols + out_proj.size),
            transcendentals=num_req * heads * SPAN,
        ),
        name="attend",
    )(page_table, req_lengths, queries, fresh, kv_pool, out_proj)


def experts_kernel(parts_ref, resid_ref, route_ref, gain_ref, in_ref, down_ref, stream_ref, total_ref):
    head = parts_ref[0]
    for k in range(1, parts_ref.shape[0]):
        head = head + parts_ref[k]
    stream = resid_ref[...].astype(jnp.float32) + head
    stream_ref[...] = stream
    mean_sq = jnp.mean(stream * stream, axis=1, keepdims=True)
    normed = (stream * lax.rsqrt(mean_sq + 1e-05) * gain_ref[...]).astype(in_ref.dtype)
    both = jnp.dot(normed, in_ref[0], preferred_element_type=jnp.float32)
    gate = both[:, :FF]
    acted = (gate / (1.0 + jnp.exp(-gate)) * both[:, FF:]).astype(down_ref.dtype)
    total_ref[...] = route_ref[...] * jnp.dot(
        acted, down_ref[0], preferred_element_type=jnp.float32
    )


def experts(parts, resid, route, norm_gain, expert_in, expert_down):
    shape = jax.ShapeDtypeStruct(resid.shape, jnp.float32)
    return pl.pallas_call(
        experts_kernel,
        out_shape=(shape, shape),
        in_specs=[VMEM] * 6,
        out_specs=(VMEM, VMEM),
        compiler_params=pltpu.CompilerParams(vmem_limit_bytes=VMEM_BYTES),
        cost_estimate=pl.CostEstimate(
            flops=2 * resid.shape[0] * (expert_in.size + expert_down.size),
            bytes_accessed=2 * (expert_in.size + expert_down.size),
            transcendentals=resid.shape[0] * FF,
        ),
        name="experts",
    )(parts, resid, route, norm_gain[None, :], expert_in, expert_down)


def forward_kernel(target_ref, landed_ref, extra_ref, send_ref):
    pieces, slot_rows, _ = landed_ref.shape
    body = slot_rows - EXTRA
    send_ref[:, body:, :] = jnp.zeros((pieces, EXTRA, LANES), send_ref.dtype)
    for s in range(pieces):
        ticket = landed_ref[s, body:, :].astype(jnp.float32)
        target = jnp.max(ticket).astype(jnp.int32)
        send_ref[target, :body, :] = landed_ref[s, :body, :]
    send_ref[target_ref[0], body:, :] = extra_ref[...]


def forward(target_rep, landed, extra):
    return pl.pallas_call(
        forward_kernel,
        out_shape=jax.ShapeDtypeStruct(landed.shape, landed.dtype),
        in_specs=[SMEM, VMEM, VMEM],
        out_specs=VMEM,
        compiler_params=pltpu.CompilerParams(vmem_limit_bytes=VMEM_BYTES),
        name="forward",
    )(target_rep, landed, extra)


def settle_kernel(leave_ref, landed_ref, hidden_ref, new_in_ref, hidden_out_ref, new_ref, arrived_ref, sem):
    del new_in_ref
    pieces, slot_rows, _ = landed_ref.shape
    body = slot_rows - EXTRA
    cols = arrived_ref.shape[2]
    rows = SPAN // pieces
    leave = leave_ref[0]
    for j in range(pieces):
        page, start = j * rows // PAGE, j * rows % PAGE
        for c in range(cols // LANES):
            arrived_ref[page, start : start + rows, c * LANES : (c + 1) * LANES] = landed_ref[
                j, c * rows : (c + 1) * rows, :
            ]
    extra = jnp.sum(landed_ref[:, body:, :].astype(jnp.float32), axis=0)
    page = jnp.max(extra[EXTRA - 1 :, :]).astype(jnp.int32)
    write = pltpu.make_async_copy(arrived_ref.at[page], new_ref.at[leave], sem)
    write.start()
    width = hidden_ref.shape[1]
    row = jnp.concatenate([extra[k : k + 1, :] for k in range(-(-width // LANES))], axis=1)
    hidden = hidden_ref[...].astype(jnp.float32)
    at_row = lax.broadcasted_iota(jnp.int32, hidden.shape, 0) == leave
    hidden_out_ref[...] = jnp.where(at_row, row[:, :width], hidden).astype(hidden_out_ref.dtype)
    write.wait()


def settle(leave_slot, landed, hidden, new_pages):
    arrived = jax.ShapeDtypeStruct((MAXP,) + new_pages.shape[1:], new_pages.dtype)
    return pl.pallas_call(
        settle_kernel,
        out_shape=(
            jax.ShapeDtypeStruct(hidden.shape, hidden.dtype),
            jax.ShapeDtypeStruct(new_pages.shape, new_pages.dtype),
            arrived,
        ),
        in_specs=[SMEM, VMEM, VMEM, ANY],
        out_specs=(VMEM, ANY, VMEM),
        scratch_shapes=[pltpu.SemaphoreType.DMA],
        input_output_aliases={3: 1},
        compiler_params=pltpu.CompilerParams(vmem_limit_bytes=VMEM_BYTES),
        name="settle",
    )(leave_slot, landed, hidden, new_pages)


def local(
    kv_pool,
    page_table,
    req_lengths,
    leave_slot,
    target_rep,
    qkv_new,
    residual_in,
    expert_ids,
    gate_weights,
    norm_gain,
    out_proj,
    expert_in,
    expert_down,
):
    pieces = lax.axis_size("rep")
    tp_size = lax.axis_size("tp")
    tp_index = lax.axis_index("tp")
    assert pieces <= 256
    send = pack(leave_slot, target_rep, page_table, req_lengths, qkv_new, kv_pool, pieces)
    landed = lax.all_to_all(send, "rep", split_axis=0, concat_axis=0, tiled=True)

    head_part, new_pages = attend(page_table, req_lengths, qkv_new, kv_pool, out_proj)
    shifts = [[(i, (i + k) % tp_size) for i in range(tp_size)] for k in range(1, tp_size)]
    parts = jnp.stack([head_part] + [lax.ppermute(head_part, "tp", shift) for shift in shifts])
    assert expert_in.shape[0] == 1
    route = jnp.sum(
        jnp.where(expert_ids == tp_index, gate_weights.astype(jnp.float32), 0.0),
        axis=1,
        keepdims=True,
    )
    stream, total = experts(parts, residual_in, route, norm_gain, expert_in, expert_down)
    width = stream.shape[1] // tp_size

    def share(values, index):
        return lax.dynamic_slice_in_dim(values, index * width, width, 1)

    mix = share(total, tp_index)
    for k, shift in enumerate(shifts, 1):
        mix = mix + lax.ppermute(share(total, (tp_index + k) % tp_size), "tp", shift)
    hidden = (share(stream, tp_index) + mix).astype(jnp.bfloat16)
    row = lax.dynamic_slice_in_dim(hidden, leave_slot[0], 1, 0)[0]
    page_number = req_lengths[leave_slot[0]] // PAGE
    row = jnp.pad(row, (0, (EXTRA - 1) * LANES - width)).reshape(EXTRA - 1, LANES)
    note = jnp.full((1, LANES), page_number.astype(hidden.dtype))
    extra = jnp.concatenate([row, note], axis=0)

    landed = lax.all_to_all(
        forward(target_rep, landed, extra), "rep", split_axis=0, concat_axis=0, tiled=True
    )
    return settle(leave_slot, landed, hidden, new_pages)


def solution(mesh):
    return jax.shard_map(
        local,
        mesh=mesh,
        in_specs=(
            P("rep", None, "tp"),
            P("rep", None),
            P("rep"),
            P("rep"),
            P("rep"),
            P("rep", "tp"),
            P("rep", None),
            P("rep", None),
            P("rep", None),
            P(),
            P("tp", None),
            P("tp", None, None),
            P("tp", None, None),
        ),
        out_specs=(P("rep", "tp"), P("rep", None, "tp"), P("rep", None, "tp")),
        check_vma=False,
    )
```

```python
import math

import jax
import jax.numpy as jnp
from jax import lax
from jax.experimental import pallas as pl
from jax.experimental.pallas import tpu as pltpu
from jax.sharding import PartitionSpec as P

QH = 24
KVH = 8
HD = 64
FF = 256
PAGE = 128
MAXP = 4
GROUP = QH // KVH
SPAN = MAXP * PAGE
LANES = 128
EXTRA = 8
VMEM_BYTES = 16 * 1024 * 1024

SMEM = pl.BlockSpec(memory_space=pltpu.SMEM)
VMEM = pl.BlockSpec(memory_space=pltpu.VMEM)
HBM = pl.BlockSpec(memory_space=pltpu.HBM)


def in_hbm(array):
    return pltpu.with_memory_space_constraint(array, pltpu.HBM)


def params():
    return pltpu.CompilerParams(vmem_limit_bytes=VMEM_BYTES)


def fresh_of(qkv, cols):
    width = (GROUP + 2) * HD
    return jnp.concatenate(
        [qkv[:, h * width + GROUP * HD : (h + 1) * width] for h in range(cols // LANES)], axis=1
    )


def blocks_of(pieces, cols):
    rows = SPAN // pieces
    return rows, [
        (j, c * rows, j * rows // PAGE, j * rows % PAGE, c * LANES)
        for j in range(pieces)
        for c in range(cols // LANES)
    ]


def put_row(ref, lead, row, fresh):
    start = pl.multiple_of(row // 16 * 16, 16)
    block = ref[lead, pl.ds(start, 16), :].astype(jnp.float32)
    at_row = lax.broadcasted_iota(jnp.int32, block.shape, 0) == row - start
    ref[lead, pl.ds(start, 16), :] = jnp.where(at_row, fresh, block).astype(ref.dtype)


def pack_kernel(
    leave_ref, target_ref, table_hbm, lens_hbm, qkv_hbm, pool_ref, send_ref,
    table_ref, lens_ref, qkv_ref, pages, small_sems, page_sems,
):
    smalls = [
        pltpu.make_async_copy(source, target, small_sems.at[i])
        for i, (source, target) in enumerate(
            [(table_hbm, table_ref), (lens_hbm, lens_ref), (qkv_hbm, qkv_ref)]
        )
    ]
    for copy in smalls:
        copy.start()
    pieces, slot_rows, _ = send_ref.shape
    body = slot_rows - EXTRA
    ticket = jnp.full((pieces, EXTRA, LANES), target_ref[0].astype(jnp.float32), jnp.float32)
    send_ref[:, body:, :] = ticket.astype(send_ref.dtype)
    smalls[0].wait()
    leave = leave_ref[0]
    copies = [
        pltpu.make_async_copy(pool_ref.at[table_ref[leave, p]], pages.at[p], page_sems.at[p])
        for p in range(MAXP)
    ]
    for copy in copies:
        copy.start()
    smalls[1].wait()
    smalls[2].wait()
    qkv = qkv_ref[...].astype(jnp.float32)
    at_row = lax.broadcasted_iota(jnp.int32, qkv.shape, 0) == leave
    qkv = jnp.sum(jnp.where(at_row, qkv, 0.0), axis=0, keepdims=True)
    fresh = fresh_of(qkv, pages.shape[2])
    length = lens_ref[leave]
    for copy in copies:
        copy.wait()
    put_row(pages, length // PAGE, length % PAGE, fresh)
    rows, blocks = blocks_of(pieces, pages.shape[2])
    for piece, at, page, start, column in blocks:
        send_ref[piece, at : at + rows, :] = pages[page, start : start + rows, column : column + LANES]


def pack(leave_slot, target_rep, page_table, req_lengths, qkv_new, kv_pool, pieces):
    cols = kv_pool.shape[2]
    slot_rows = SPAN // pieces * (cols // LANES) + EXTRA
    return pl.pallas_call(
        pack_kernel,
        out_shape=pltpu.VMEM((pieces, slot_rows, LANES), kv_pool.dtype),
        in_specs=[SMEM, SMEM] + [HBM] * 4,
        out_specs=VMEM,
        scratch_shapes=[
            pltpu.SMEM(page_table.shape, page_table.dtype),
            pltpu.SMEM(req_lengths.shape, req_lengths.dtype),
            pltpu.VMEM(qkv_new.shape, qkv_new.dtype),
            pltpu.VMEM((MAXP, PAGE, cols), kv_pool.dtype),
            pltpu.SemaphoreType.DMA((3,)),
            pltpu.SemaphoreType.DMA((MAXP,)),
        ],
        compiler_params=params(),
        name="pack",
    )(leave_slot, target_rep, *map(in_hbm, (page_table, req_lengths, qkv_new, kv_pool)))


def attend_kernel(table_ref, lens_ref, qkv_ref, pool_ref, proj_ref, head_ref, new_ref, stage, sems):
    num_req = qkv_ref.shape[0]
    cols = pool_ref.shape[2]
    heads = cols // LANES
    rows = -(-heads * GROUP // 16) * 16
    width = (GROUP + 2) * HD
    qkv = qkv_ref[...].astype(jnp.float32)
    fresh = fresh_of(qkv, cols)

    writes = []
    for r in range(num_req):
        length = lens_ref[r]
        stage[r] = pool_ref[table_ref[r, length // PAGE]]
        put_row(stage, r, length % PAGE, fresh[r : r + 1, :])
        write = pltpu.make_async_copy(stage.at[r], new_ref.at[r], sems.at[r])
        write.start()
        writes.append(write)

    queries = []
    for r in range(num_req):
        blocks = []
        for h in range(heads):
            block = jnp.concatenate(
                [qkv[r : r + 1, h * width + g * HD : h * width + (g + 2) * HD] for g in range(GROUP)], axis=0
            )
            lane = lax.broadcasted_iota(jnp.int32, block.shape, 1)
            block = jnp.where(lane < HD, block, 0.0)
            parts = [jnp.zeros_like(block)] * heads
            parts[h] = block
            blocks.append(jnp.concatenate(parts, axis=1))
        if rows > heads * GROUP:
            blocks.append(jnp.zeros((rows - heads * GROUP, cols), jnp.float32))
        queries.append(jnp.concatenate(blocks, axis=0))

    scores, masks = [], []
    for r in range(num_req):
        length = lens_ref[r]
        query = queries[r].astype(pool_ref.dtype)
        score = jnp.concatenate(
            [
                lax.dot_general(
                    query, pool_ref[table_ref[r, p]], (((1,), (1,)), ((), ())),
                    preferred_element_type=jnp.float32,
                )
                for p in range(MAXP)
            ],
            axis=1,
        )
        own = jnp.sum(queries[r] * fresh[r : r + 1, :], axis=1, keepdims=True)
        positions = lax.broadcasted_iota(jnp.int32, score.shape, 1)
        score = jnp.where(positions == length, own, score) * (1.0 / math.sqrt(HD))
        scores.append(jnp.where(positions <= length, score, -jnp.inf))
        masks.append(positions == length)
    score = jnp.concatenate(scores, axis=0)
    mask = jnp.concatenate(masks, axis=0)
    weights = jnp.exp(score - jnp.max(score, axis=1, keepdims=True))
    probs = (weights / jnp.sum(weights, axis=1, keepdims=True)).astype(pool_ref.dtype).astype(jnp.float32)
    own = jnp.sum(jnp.where(mask, probs, 0.0), axis=1, keepdims=True)
    probs = jnp.where(mask, 0.0, probs).astype(pool_ref.dtype)

    attn = []
    for r in range(num_req):
        out = own[r * rows : (r + 1) * rows, :] * fresh[r : r + 1, :]
        for p in range(MAXP):
            out = out + jnp.dot(
                probs[r * rows : (r + 1) * rows, p * PAGE : (p + 1) * PAGE], pool_ref[table_ref[r, p]],
                preferred_element_type=jnp.float32,
            )
        attn.append(
            jnp.concatenate(
                [
                    out[i : i + 1, i // GROUP * LANES + HD : (i // GROUP + 1) * LANES]
                    for i in range(heads * GROUP)
                ],
                axis=1,
            )
        )
    attn = jnp.concatenate(attn, axis=0).astype(proj_ref.dtype)
    head_ref[...] = jnp.dot(attn, proj_ref[...], preferred_element_type=jnp.float32)
    for write in writes:
        write.wait()


def attend(page_table, req_lengths, qkv_new, kv_pool, out_proj):
    num_req = qkv_new.shape[0]
    cols = kv_pool.shape[2]
    return pl.pallas_call(
        attend_kernel,
        out_shape=(
            jax.ShapeDtypeStruct((num_req, out_proj.shape[1]), jnp.float32),
            jax.ShapeDtypeStruct((num_req, PAGE, cols), kv_pool.dtype),
        ),
        in_specs=[SMEM, SMEM, VMEM, VMEM, VMEM],
        out_specs=(VMEM, HBM),
        scratch_shapes=[
            pltpu.VMEM((num_req, PAGE, cols), kv_pool.dtype),
            pltpu.SemaphoreType.DMA((num_req,)),
        ],
        compiler_params=params(),
        cost_estimate=pl.CostEstimate(
            flops=2 * num_req * (2 * 16 * SPAN * cols + out_proj.size),
            bytes_accessed=2 * (num_req * SPAN * cols + out_proj.size),
            transcendentals=num_req * 16 * SPAN,
        ),
        name="attend",
    )(page_table, req_lengths, qkv_new, kv_pool, out_proj)


def experts_kernel(
    index_ref, ids_ref, gates_ref, resid_ref, gain_ref, in_ref, down_ref, *parts_refs
):
    *parts_refs, stream_ref, total_ref = parts_refs
    head = parts_refs[0][...]
    for part in parts_refs[1:]:
        head = head + part[...]
    stream = resid_ref[...].astype(jnp.float32) + head
    stream_ref[...] = stream
    mean_sq = jnp.mean(stream * stream, axis=1, keepdims=True)
    normed = (stream * lax.rsqrt(mean_sq + 1e-05) * gain_ref[...]).astype(in_ref.dtype)
    both = jnp.dot(normed, in_ref[0], preferred_element_type=jnp.float32)
    gate = both[:, :FF]
    acted = (gate / (1.0 + jnp.exp(-gate)) * both[:, FF:]).astype(down_ref.dtype)
    chosen = ids_ref[...] == index_ref[0]
    route = jnp.sum(
        jnp.where(chosen, gates_ref[...].astype(jnp.float32), 0.0), axis=1, keepdims=True
    )
    total_ref[...] = route * jnp.dot(acted, down_ref[0], preferred_element_type=jnp.float32)


def experts(tp_index, expert_ids, gate_weights, resid, norm_gain, expert_in, expert_down, parts):
    shape = jax.ShapeDtypeStruct(resid.shape, jnp.float32)
    return pl.pallas_call(
        experts_kernel,
        out_shape=(shape, shape),
        in_specs=[SMEM] + [VMEM] * (6 + len(parts)),
        out_specs=(VMEM, VMEM),
        compiler_params=params(),
        cost_estimate=pl.CostEstimate(
            flops=2 * resid.shape[0] * (expert_in.size + expert_down.size),
            bytes_accessed=2 * (expert_in.size + expert_down.size),
            transcendentals=resid.shape[0] * FF,
        ),
        name="experts",
    )(
        tp_index[None], expert_ids, gate_weights, resid, norm_gain[None, :], expert_in, expert_down, *parts
    )


def forward_kernel(target_ref, landed_ref, extra_ref, send_ref):
    pieces, slot_rows, _ = landed_ref.shape
    body = slot_rows - EXTRA
    send_ref[:, body:, :] = jnp.zeros((pieces, EXTRA, LANES), send_ref.dtype)
    for s in range(pieces):
        target = jnp.max(landed_ref[s, body:, :].astype(jnp.float32)).astype(jnp.int32)
        send_ref[target, :body, :] = landed_ref[s, :body, :]
    send_ref[target_ref[0], body:, :] = extra_ref[...]


def forward(target_rep, landed, extra):
    return pl.pallas_call(
        forward_kernel,
        out_shape=pltpu.VMEM(landed.shape, landed.dtype),
        in_specs=[SMEM, VMEM, VMEM],
        out_specs=VMEM,
        compiler_params=params(),
        name="forward",
    )(target_rep, landed, extra)


def settle_kernel(
    slot_ref, landed_ref, hidden_ref, new_in_ref, hidden_out_ref, new_ref, arrived_ref, pages, sems
):
    del new_in_ref
    pieces, slot_rows, _ = landed_ref.shape
    body = slot_rows - EXTRA
    rows, blocks = blocks_of(pieces, pages.shape[2])
    for piece, at, page, start, column in blocks:
        pages[page, start : start + rows, column : column + LANES] = landed_ref[piece, at : at + rows, :]
    all_pages = pltpu.make_async_copy(pages, arrived_ref, sems.at[0])
    all_pages.start()
    extra = jnp.sum(landed_ref[:, body:, :].astype(jnp.float32), axis=0)
    page = jnp.max(extra[EXTRA - 1 :, :]).astype(jnp.int32)
    leave = jnp.max(slot_ref[...]).astype(jnp.int32)
    new_page = pltpu.make_async_copy(pages.at[page], new_ref.at[leave], sems.at[1])
    new_page.start()
    width = hidden_ref.shape[1]
    row = jnp.concatenate([extra[k : k + 1, :] for k in range(-(-width // LANES))], axis=1)
    hidden = hidden_ref[...].astype(jnp.float32)
    at_row = lax.broadcasted_iota(jnp.int32, hidden.shape, 0) == leave
    hidden_out_ref[...] = jnp.where(at_row, row[:, :width], hidden).astype(hidden_out_ref.dtype)
    all_pages.wait()
    new_page.wait()


def settle(slot, landed, hidden, new_pages):
    arrived = (MAXP,) + new_pages.shape[1:]
    return pl.pallas_call(
        settle_kernel,
        out_shape=(
            jax.ShapeDtypeStruct(hidden.shape, hidden.dtype),
            jax.ShapeDtypeStruct(new_pages.shape, new_pages.dtype),
            jax.ShapeDtypeStruct(arrived, new_pages.dtype),
        ),
        in_specs=[VMEM, VMEM, VMEM, HBM],
        out_specs=(VMEM, HBM, HBM),
        scratch_shapes=[pltpu.VMEM(arrived, new_pages.dtype), pltpu.SemaphoreType.DMA((2,))],
        input_output_aliases={3: 1},
        compiler_params=params(),
        name="settle",
    )(slot, landed, hidden, new_pages)


def local(
    kv_pool,
    page_table,
    req_lengths,
    leave_slot,
    target_rep,
    qkv_new,
    residual_in,
    expert_ids,
    gate_weights,
    norm_gain,
    out_proj,
    expert_in,
    expert_down,
):
    pieces = lax.axis_size("rep")
    tp_size = lax.axis_size("tp")
    tp_index = lax.axis_index("tp")
    assert pieces <= 256

    def exchange(packet):
        return lax.all_to_all(packet, "rep", split_axis=0, concat_axis=0, tiled=True)

    send = pack(leave_slot, target_rep, page_table, req_lengths, qkv_new, kv_pool, pieces)
    send, qkv_new = lax.optimization_barrier((send, qkv_new))
    landed = exchange(send)

    head_part, new_pages = attend(page_table, req_lengths, qkv_new, kv_pool, out_proj)
    shifts = [[(i, (i + k) % tp_size) for i in range(tp_size)] for k in range(1, tp_size)]
    parts = [head_part] + [lax.ppermute(head_part, "tp", shift) for shift in shifts]
    assert expert_in.shape[0] == 1
    stream, total = experts(
        tp_index, expert_ids, gate_weights, residual_in, norm_gain, expert_in, expert_down, parts
    )
    width = stream.shape[1] // tp_size

    def share(values, index):
        return lax.dynamic_slice_in_dim(values, index * width, width, 1)

    mix = share(total, tp_index)
    for k, shift in enumerate(shifts, 1):
        mix = mix + lax.ppermute(share(total, (tp_index + k) % tp_size), "tp", shift)
    hidden = (share(stream, tp_index) + mix).astype(jnp.bfloat16)
    row = lax.dynamic_slice_in_dim(hidden, leave_slot[0], 1, 0)[0]
    row = jnp.pad(row, (0, (EXTRA - 1) * LANES - width)).reshape(EXTRA - 1, LANES)
    page_number = (req_lengths[leave_slot[0]] // PAGE).astype(hidden.dtype)
    extra = jnp.concatenate([row, jnp.full((1, LANES), page_number)], axis=0)
    slot = jnp.full((EXTRA, LANES), leave_slot[0].astype(jnp.float32))

    landed = exchange(forward(target_rep, landed, extra))
    return settle(slot, landed, hidden, new_pages)


def solution(mesh):
    return jax.shard_map(
        local,
        mesh=mesh,
        in_specs=(
            P("rep", None, "tp"),
            P("rep", None),
            P("rep"),
            P("rep"),
            P("rep"),
            P("rep", "tp"),
            P("rep", None),
            P("rep", None),
            P("rep", None),
            P(),
            P("tp", None),
            P("tp", None, None),
            P("tp", None, None),
        ),
        out_specs=(P("rep", "tp"), P("rep", None, "tp"), P("rep", None, "tp")),
        check_vma=False,
    )
```

```python
import functools
import math

import jax
import jax.numpy as jnp
from jax import lax
from jax.experimental import pallas as pl
from jax.experimental.pallas import tpu as pltpu
from jax.sharding import PartitionSpec as P

QH = 24
KVH = 8
HD = 64
FF = 256
PAGE = 128
MAXP = 4
GROUP = QH // KVH
SPAN = MAXP * PAGE
LANES = 128
EXTRA = 8
VMEM_BYTES = 16 * 1024 * 1024
SPREAD = {16: (11, 8, 3, 14, 13, 12, 4, 10, 9, 7, 1, 0, 2, 15, 5, 6)}
DELIVER = {16: (10, 9, 3, 13, 12, 7, 2, 8, 14, 15, 4, 0, 6, 11, 1, 5)}

SMEM = pl.BlockSpec(memory_space=pltpu.SMEM)
VMEM = pl.BlockSpec(memory_space=pltpu.VMEM)
HBM = pl.BlockSpec(memory_space=pltpu.HBM)


def in_hbm(array):
    return pltpu.with_memory_space_constraint(array, pltpu.HBM)


def params():
    return pltpu.CompilerParams(vmem_limit_bytes=VMEM_BYTES)


def peers_of(orders, count):
    return orders.get(count, tuple(range(count)))


def place_of(replica, peers):
    place = replica
    for k, peer in enumerate(peers):
        place = jnp.where(replica == peer, k, place)
    return place


def fresh_of(qkv, cols):
    width = (GROUP + 2) * HD
    return jnp.concatenate(
        [qkv[:, h * width + GROUP * HD : (h + 1) * width] for h in range(cols // LANES)], axis=1
    )


def put_row(ref, lead, row, fresh):
    start = pl.multiple_of(row // 16 * 16, 16)
    block = ref[lead, pl.ds(start, 16), :].astype(jnp.float32)
    at_row = lax.broadcasted_iota(jnp.int32, block.shape, 0) == row - start
    ref[lead, pl.ds(start, 16), :] = jnp.where(at_row, fresh, block).astype(ref.dtype)


def pack_kernel(
    pieces, leave_ref, target_ref, table_hbm, lens_hbm, qkv_hbm, pool_ref, send_ref, taken_ref,
    table_ref, lens_ref, qkv_ref, pages, small_sems, page_sems, send_sems,
):
    smalls = [
        pltpu.make_async_copy(source, target, small_sems.at[i])
        for i, (source, target) in enumerate(
            [(table_hbm, table_ref), (lens_hbm, lens_ref), (qkv_hbm, qkv_ref)]
        )
    ]
    for copy in smalls:
        copy.start()
    smalls[0].wait()
    leave = leave_ref[0]
    copies = [
        pltpu.make_async_copy(pool_ref.at[table_ref[leave, p]], pages.at[p], page_sems.at[p])
        for p in range(MAXP)
    ]
    for copy in copies:
        copy.start()
    cols = pages.shape[2]
    rows = SPAN // pieces
    ticket = place_of(target_ref[0], peers_of(DELIVER, pieces)).astype(jnp.float32)
    smalls[1].wait()
    smalls[2].wait()
    qkv = qkv_ref[...].astype(jnp.float32)
    at_row = lax.broadcasted_iota(jnp.int32, qkv.shape, 0) == leave
    qkv = jnp.sum(jnp.where(at_row, qkv, 0.0), axis=0, keepdims=True)
    fresh = fresh_of(qkv, cols)
    length = lens_ref[leave]
    taken = jnp.zeros((16, LANES), jnp.float32)
    row_in = lax.broadcasted_iota(jnp.int32, taken.shape, 0)
    lane = lax.broadcasted_iota(jnp.int32, taken.shape, 1)
    sends = []
    for p in range(MAXP):
        copies[p].wait()

        @pl.when(length // PAGE == p)
        def _():
            put_row(pages, p, length % PAGE, fresh)

        for j in range(p * pieces // MAXP, (p + 1) * pieces // MAXP):
            last = (j + 1) * rows - 1 - p * PAGE
            start = last // 16 * 16
            block = pages[p, start : start + 16, :LANES].astype(jnp.float32)
            at = jnp.logical_and(row_in == last - start, lane == j)
            taken = taken + jnp.where(at, block, 0.0)
            pages[p, start : start + 16, :LANES] = jnp.where(at, ticket, block).astype(pages.dtype)
        sends.append(pltpu.make_async_copy(pages.at[p], send_ref.at[p], send_sems.at[p]))
        sends[p].start()
    taken_ref[...] = jnp.sum(taken, axis=0, keepdims=True)
    for send in sends:
        send.wait()


def pack(leave_slot, target_rep, page_table, req_lengths, qkv_new, kv_pool, pieces):
    cols = kv_pool.shape[2]
    assert pieces % MAXP == 0 and pieces <= LANES
    return pl.pallas_call(
        functools.partial(pack_kernel, pieces),
        out_shape=(
            pltpu.HBM((MAXP, PAGE, cols), kv_pool.dtype),
            jax.ShapeDtypeStruct((1, LANES), jnp.float32),
        ),
        in_specs=[SMEM, SMEM] + [HBM] * 4,
        out_specs=(HBM, VMEM),
        scratch_shapes=[
            pltpu.SMEM(page_table.shape, page_table.dtype),
            pltpu.SMEM(req_lengths.shape, req_lengths.dtype),
            pltpu.VMEM(qkv_new.shape, qkv_new.dtype),
            pltpu.VMEM((MAXP, PAGE, cols), kv_pool.dtype),
            pltpu.SemaphoreType.DMA((3,)),
            pltpu.SemaphoreType.DMA((MAXP,)),
            pltpu.SemaphoreType.DMA((MAXP,)),
        ],
        compiler_params=params(),
        name="pack",
    )(leave_slot, target_rep, *map(in_hbm, (page_table, req_lengths, qkv_new, kv_pool)))


def attend_kernel(
    leave_ref, table_ref, lens_ref, qkv_ref, pool_ref, proj_hbm, head_ref, new_ref, note_ref,
    stage, proj_ref, sems, proj_sem,
):
    proj_read = pltpu.make_async_copy(proj_hbm, proj_ref, proj_sem)
    proj_read.start()
    note = (lens_ref[leave_ref[0]] // PAGE).astype(jnp.float32)
    note_ref[...] = jnp.full(note_ref.shape, note, jnp.float32)
    num_req = qkv_ref.shape[0]
    cols = pool_ref.shape[2]
    heads = cols // LANES
    rows = -(-heads * GROUP // 16) * 16
    width = (GROUP + 2) * HD
    qkv = qkv_ref[...].astype(jnp.float32)
    fresh = fresh_of(qkv, cols)

    writes = []
    for r in range(num_req):
        length = lens_ref[r]
        stage[r] = pool_ref[table_ref[r, length // PAGE]]
        put_row(stage, r, length % PAGE, fresh[r : r + 1, :])
        write = pltpu.make_async_copy(stage.at[r], new_ref.at[r], sems.at[r])
        write.start()
        writes.append(write)

    queries = []
    for r in range(num_req):
        blocks = []
        for h in range(heads):
            block = jnp.concatenate(
                [qkv[r : r + 1, h * width + g * HD : h * width + (g + 2) * HD] for g in range(GROUP)], axis=0
            )
            lane = lax.broadcasted_iota(jnp.int32, block.shape, 1)
            block = jnp.where(lane < HD, block, 0.0)
            parts = [jnp.zeros_like(block)] * heads
            parts[h] = block
            blocks.append(jnp.concatenate(parts, axis=1))
        if rows > heads * GROUP:
            blocks.append(jnp.zeros((rows - heads * GROUP, cols), jnp.float32))
        queries.append(jnp.concatenate(blocks, axis=0))

    scores, masks = [], []
    for r in range(num_req):
        length = lens_ref[r]
        query = queries[r].astype(pool_ref.dtype)
        score = jnp.concatenate(
            [
                lax.dot_general(
                    query, pool_ref[table_ref[r, p]], (((1,), (1,)), ((), ())),
                    preferred_element_type=jnp.float32,
                )
                for p in range(MAXP)
            ],
            axis=1,
        )
        own = jnp.sum(queries[r] * fresh[r : r + 1, :], axis=1, keepdims=True)
        positions = lax.broadcasted_iota(jnp.int32, score.shape, 1)
        score = jnp.where(positions == length, own, score) * (1.0 / math.sqrt(HD))
        scores.append(jnp.where(positions <= length, score, -jnp.inf))
        masks.append(positions == length)
    score = jnp.concatenate(scores, axis=0)
    mask = jnp.concatenate(masks, axis=0)
    weights = jnp.exp(score - jnp.max(score, axis=1, keepdims=True))
    probs = (weights / jnp.sum(weights, axis=1, keepdims=True)).astype(pool_ref.dtype).astype(jnp.float32)
    own = jnp.sum(jnp.where(mask, probs, 0.0), axis=1, keepdims=True)
    probs = jnp.where(mask, 0.0, probs).astype(pool_ref.dtype)

    attn = []
    for r in range(num_req):
        out = own[r * rows : (r + 1) * rows, :] * fresh[r : r + 1, :]
        for p in range(MAXP):
            out = out + jnp.dot(
                probs[r * rows : (r + 1) * rows, p * PAGE : (p + 1) * PAGE], pool_ref[table_ref[r, p]],
                preferred_element_type=jnp.float32,
            )
        attn.append(
            jnp.concatenate(
                [
                    out[i : i + 1, i // GROUP * LANES + HD : (i // GROUP + 1) * LANES]
                    for i in range(heads * GROUP)
                ],
                axis=1,
            )
        )
    attn = jnp.concatenate(attn, axis=0).astype(proj_ref.dtype)
    proj_read.wait()
    head_ref[...] = jnp.dot(attn, proj_ref[...], preferred_element_type=jnp.float32)
    for write in writes:
        write.wait()


def attend(leave_slot, page_table, req_lengths, qkv_new, kv_pool, out_proj):
    num_req = qkv_new.shape[0]
    cols = kv_pool.shape[2]
    return pl.pallas_call(
        attend_kernel,
        out_shape=(
            jax.ShapeDtypeStruct((num_req, out_proj.shape[1]), jnp.float32),
            jax.ShapeDtypeStruct((num_req, PAGE, cols), kv_pool.dtype),
            jax.ShapeDtypeStruct((1, LANES), jnp.float32),
        ),
        in_specs=[SMEM, SMEM, SMEM, VMEM, VMEM, HBM],
        out_specs=(VMEM, HBM, VMEM),
        scratch_shapes=[
            pltpu.VMEM((num_req, PAGE, cols), kv_pool.dtype),
            pltpu.VMEM(out_proj.shape, out_proj.dtype),
            pltpu.SemaphoreType.DMA((num_req,)),
            pltpu.SemaphoreType.DMA,
        ],
        compiler_params=params(),
        cost_estimate=pl.CostEstimate(
            flops=2 * num_req * (2 * 16 * SPAN * cols + out_proj.size),
            bytes_accessed=2 * (num_req * SPAN * cols + out_proj.size),
            transcendentals=num_req * 16 * SPAN,
        ),
        name="attend",
    )(leave_slot, page_table, req_lengths, qkv_new, kv_pool, in_hbm(out_proj))


def experts_kernel(
    index_ref, ids_ref, gates_ref, resid_ref, gain_ref, in_ref, down_ref, *parts_refs
):
    *parts_refs, stream_ref, total_ref = parts_refs
    head = parts_refs[0][...]
    for part in parts_refs[1:]:
        head = head + part[...]
    stream = resid_ref[...].astype(jnp.float32) + head
    stream_ref[...] = stream
    mean_sq = jnp.mean(stream * stream, axis=1, keepdims=True)
    normed = (stream * lax.rsqrt(mean_sq + 1e-05) * gain_ref[...]).astype(in_ref.dtype)
    both = jnp.dot(normed, in_ref[0], preferred_element_type=jnp.float32)
    gate = both[:, :FF]
    acted = (gate / (1.0 + jnp.exp(-gate)) * both[:, FF:]).astype(down_ref.dtype)
    chosen = ids_ref[...] == index_ref[0]
    route = jnp.sum(
        jnp.where(chosen, gates_ref[...].astype(jnp.float32), 0.0), axis=1, keepdims=True
    )
    total_ref[...] = route * jnp.dot(acted, down_ref[0], preferred_element_type=jnp.float32)


def experts(tp_index, expert_ids, gate_weights, resid, norm_gain, expert_in, expert_down, parts):
    shape = jax.ShapeDtypeStruct(resid.shape, jnp.float32)
    return pl.pallas_call(
        experts_kernel,
        out_shape=(shape, shape),
        in_specs=[SMEM] + [VMEM] * (6 + len(parts)),
        out_specs=(VMEM, VMEM),
        compiler_params=params(),
        cost_estimate=pl.CostEstimate(
            flops=2 * resid.shape[0] * (expert_in.size + expert_down.size),
            bytes_accessed=2 * (expert_in.size + expert_down.size),
            transcendentals=resid.shape[0] * FF,
        ),
        name="experts",
    )(
        tp_index[None], expert_ids, gate_weights, resid, norm_gain[None, :], expert_in, expert_down, *parts
    )


def forward_kernel(
    leave_ref, target_ref, index_ref, landed_ref, hidden_ref, note_ref, taken_ref, send_ref
):
    pieces, rows, cols = landed_ref.shape
    body = rows * cols // LANES
    send_ref[:, body:, :] = jnp.zeros((pieces, EXTRA, LANES), send_ref.dtype)
    own = place_of(index_ref[0], peers_of(SPREAD, pieces))
    lane = lax.broadcasted_iota(jnp.int32, (1, LANES), 1)
    for s in range(pieces):
        last = landed_ref[s, rows - 1 :, :LANES].astype(jnp.float32)
        place = jnp.max(jnp.where(lane == own, last, 0.0)).astype(jnp.int32)
        for c in range(cols // LANES):
            send_ref[place, c * rows : (c + 1) * rows, :] = landed_ref[s, :, c * LANES : (c + 1) * LANES]
    hidden = hidden_ref[...].astype(jnp.float32)
    at_row = lax.broadcasted_iota(jnp.int32, hidden.shape, 0) == leave_ref[0]
    row = jnp.sum(jnp.where(at_row, hidden, 0.0), axis=0, keepdims=True)
    spare = (EXTRA - 2) * LANES - row.shape[1]
    if spare:
        row = jnp.concatenate([row, jnp.zeros((1, spare), jnp.float32)], axis=1)
    lines = [row[:, k * LANES : (k + 1) * LANES] for k in range(EXTRA - 2)]
    place = place_of(target_ref[0], peers_of(DELIVER, pieces))
    extra = jnp.concatenate(lines + [taken_ref[...], note_ref[...]], axis=0)
    send_ref[place, body:, :] = extra.astype(send_ref.dtype)


def forward(leave_slot, target_rep, rep_index, landed, hidden, note, taken):
    pieces, rows, cols = landed.shape
    return pl.pallas_call(
        forward_kernel,
        out_shape=jax.ShapeDtypeStruct((pieces, rows * cols // LANES + EXTRA, LANES), landed.dtype),
        in_specs=[SMEM, SMEM, SMEM, VMEM, VMEM, VMEM, VMEM],
        out_specs=VMEM,
        compiler_params=params(),
        name="forward",
    )(leave_slot, target_rep, rep_index, landed, hidden, note, taken)


def settle_kernel(
    leave_ref, landed_ref, hidden_ref, new_in_ref, hidden_out_ref, new_ref, arrived_ref,
    pages, mixed, page_sems, new_sem, hidden_sem,
):
    del new_in_ref
    pieces, slot_rows, _ = landed_ref.shape
    body = slot_rows - EXTRA
    cols = pages.shape[2]
    rows = SPAN // pieces
    leave = leave_ref[0]
    extra = jnp.sum(landed_ref[:, body:, :].astype(jnp.float32), axis=0)
    taken = extra[EXTRA - 2 : EXTRA - 1, :]
    spread, deliver = peers_of(SPREAD, pieces), peers_of(DELIVER, pieces)
    row_in = lax.broadcasted_iota(jnp.int32, (rows, LANES), 0)
    lane = lax.broadcasted_iota(jnp.int32, (rows, LANES), 1)
    writes = []
    for p in range(MAXP):
        for j in range(p * pieces // MAXP, (p + 1) * pieces // MAXP):
            slot = deliver.index(spread[j])
            start = j * rows - p * PAGE
            for c in range(cols // LANES):
                block = landed_ref[slot, c * rows : (c + 1) * rows, :]
                if c == 0:
                    at = jnp.logical_and(row_in == rows - 1, lane == j)
                    block = jnp.where(at, taken, block.astype(jnp.float32)).astype(pages.dtype)
                pages[p, start : start + rows, c * LANES : (c + 1) * LANES] = block
        writes.append(pltpu.make_async_copy(pages.at[p], arrived_ref.at[p], page_sems.at[p]))
        writes[p].start()
    page = jnp.max(extra[EXTRA - 1 :, :]).astype(jnp.int32)
    writes.append(pltpu.make_async_copy(pages.at[page], new_ref.at[leave], new_sem))
    writes[-1].start()
    width = hidden_ref.shape[1]
    row = jnp.concatenate([extra[k : k + 1, :] for k in range(-(-width // LANES))], axis=1)
    hidden = hidden_ref[...].astype(jnp.float32)
    at_row = lax.broadcasted_iota(jnp.int32, hidden.shape, 0) == leave
    mixed[...] = jnp.where(at_row, row[:, :width], hidden).astype(mixed.dtype)
    writes.append(pltpu.make_async_copy(mixed, hidden_out_ref, hidden_sem))
    writes[-1].start()
    for write in writes:
        write.wait()


def settle(leave_slot, landed, hidden, new_pages):
    arrived = (MAXP,) + new_pages.shape[1:]
    return pl.pallas_call(
        settle_kernel,
        out_shape=(
            jax.ShapeDtypeStruct(hidden.shape, hidden.dtype),
            jax.ShapeDtypeStruct(new_pages.shape, new_pages.dtype),
            jax.ShapeDtypeStruct(arrived, new_pages.dtype),
        ),
        in_specs=[SMEM, VMEM, VMEM, HBM],
        out_specs=(HBM, HBM, HBM),
        scratch_shapes=[
            pltpu.VMEM(arrived, new_pages.dtype),
            pltpu.VMEM(hidden.shape, hidden.dtype),
            pltpu.SemaphoreType.DMA((MAXP,)),
            pltpu.SemaphoreType.DMA,
            pltpu.SemaphoreType.DMA,
        ],
        input_output_aliases={3: 1},
        compiler_params=params(),
        name="settle",
    )(leave_slot, landed, hidden, new_pages)


def local(
    kv_pool,
    page_table,
    req_lengths,
    leave_slot,
    target_rep,
    qkv_new,
    residual_in,
    expert_ids,
    gate_weights,
    norm_gain,
    out_proj,
    expert_in,
    expert_down,
):
    pieces = lax.axis_size("rep")
    tp_size = lax.axis_size("tp")
    tp_index = lax.axis_index("tp")

    def exchange(packet, orders):
        return lax.all_to_all(
            packet, "rep", split_axis=0, concat_axis=0, tiled=True,
            axis_index_groups=[peers_of(orders, pieces)],
        )

    send, taken = pack(leave_slot, target_rep, page_table, req_lengths, qkv_new, kv_pool, pieces)
    send, qkv_new = lax.optimization_barrier((send, qkv_new))
    landed = exchange(send.reshape(pieces, SPAN // pieces, kv_pool.shape[2]), SPREAD)

    head_part, new_pages, note = attend(
        leave_slot, page_table, req_lengths, qkv_new, kv_pool, out_proj
    )
    shifts = [[(i, (i + k) % tp_size) for i in range(tp_size)] for k in range(1, tp_size)]
    parts = [head_part] + [lax.ppermute(head_part, "tp", shift) for shift in shifts]
    assert expert_in.shape[0] == 1
    stream, total = experts(
        tp_index, expert_ids, gate_weights, residual_in, norm_gain, expert_in, expert_down, parts
    )
    width = stream.shape[1] // tp_size

    def share(values, index):
        return lax.dynamic_slice_in_dim(values, index * width, width, 1)

    mix = share(total, tp_index)
    for k, shift in enumerate(shifts, 1):
        mix = mix + lax.ppermute(share(total, (tp_index + k) % tp_size), "tp", shift)
    hidden = (share(stream, tp_index) + mix).astype(jnp.bfloat16)
    rep_index = lax.axis_index("rep")[None]
    landed = exchange(
        forward(leave_slot, target_rep, rep_index, landed, hidden, note, taken), DELIVER
    )
    return settle(leave_slot, landed, hidden, new_pages)


def solution(mesh):
    return jax.shard_map(
        local,
        mesh=mesh,
        in_specs=(
            P("rep", None, "tp"),
            P("rep", None),
            P("rep"),
            P("rep"),
            P("rep"),
            P("rep", "tp"),
            P("rep", None),
            P("rep", None),
            P("rep", None),
            P(),
            P("tp", None),
            P("tp", None, None),
            P("tp", None, None),
        ),
        out_specs=(P("rep", "tp"), P("rep", None, "tp"), P("rep", None, "tp")),
        check_vma=False,
    )
```

```python
import functools
import math

import jax
import jax.numpy as jnp
from jax import lax
from jax.experimental import pallas as pl
from jax.experimental.pallas import tpu as pltpu
from jax.sharding import PartitionSpec as P

QH = 24
KVH = 8
HD = 64
FF = 256
PAGE = 128
MAXP = 4
GROUP = QH // KVH
SPAN = MAXP * PAGE
LANES = 128
EXTRA = 8
VMEM_BYTES = 16 * 1024 * 1024
ORDERS = {(16, 2): (
    (0, 8, 2, 3, 4, 5, 6, 13, 1, 15, 10, 11, 14, 7, 12, 9),
    (10, 9, 8, 11, 4, 15, 12, 0, 2, 3, 1, 13, 14, 7, 6, 5),
)}

SMEM = pl.BlockSpec(memory_space=pltpu.SMEM)
VMEM = pl.BlockSpec(memory_space=pltpu.VMEM)
HBM = pl.BlockSpec(memory_space=pltpu.HBM)


def in_hbm(array):
    return pltpu.with_memory_space_constraint(array, pltpu.HBM)


def params():
    return pltpu.CompilerParams(vmem_limit_bytes=VMEM_BYTES)


def place_of(replica, tp_index, mesh_shape):
    place = replica
    for core, peers in enumerate(ORDERS.get(mesh_shape, ())):
        for k, peer in enumerate(peers):
            hit = jnp.logical_and(replica == peer, tp_index == core)
            place = jnp.where(hit, k, place)
    return place


def fresh_of(qkv, cols):
    width = (GROUP + 2) * HD
    return jnp.concatenate(
        [qkv[:, h * width + GROUP * HD : (h + 1) * width] for h in range(cols // LANES)], axis=1
    )


def put_row(ref, lead, row, fresh):
    start = pl.multiple_of(row // 16 * 16, 16)
    block = ref[lead, pl.ds(start, 16), :].astype(jnp.float32)
    at_row = lax.broadcasted_iota(jnp.int32, block.shape, 0) == row - start
    ref[lead, pl.ds(start, 16), :] = jnp.where(at_row, fresh, block).astype(ref.dtype)


def pack_kernel(
    mesh_shape, leave_ref, target_ref, tp_ref, table_hbm, lens_hbm, qkv_hbm, pool_ref, send_ref, taken_ref,
    table_ref, lens_ref, qkv_ref, pages, small_sems, page_sems, send_sems,
):
    smalls = [
        pltpu.make_async_copy(source, target, small_sems.at[i])
        for i, (source, target) in enumerate(
            [(table_hbm, table_ref), (lens_hbm, lens_ref), (qkv_hbm, qkv_ref)]
        )
    ]
    for copy in smalls:
        copy.start()
    smalls[0].wait()
    leave = leave_ref[0]
    copies = [
        pltpu.make_async_copy(pool_ref.at[table_ref[leave, p]], pages.at[p], page_sems.at[p])
        for p in range(MAXP)
    ]
    for copy in copies:
        copy.start()
    cols = pages.shape[2]
    pieces = mesh_shape[0]
    rows = SPAN // pieces
    ticket = place_of(target_ref[0], tp_ref[0], mesh_shape).astype(jnp.float32)
    smalls[1].wait()
    smalls[2].wait()
    qkv = qkv_ref[...].astype(jnp.float32)
    at_row = lax.broadcasted_iota(jnp.int32, qkv.shape, 0) == leave
    qkv = jnp.sum(jnp.where(at_row, qkv, 0.0), axis=0, keepdims=True)
    fresh = fresh_of(qkv, cols)
    length = lens_ref[leave]
    taken = jnp.zeros((16, LANES), jnp.float32)
    row_in = lax.broadcasted_iota(jnp.int32, taken.shape, 0)
    lane = lax.broadcasted_iota(jnp.int32, taken.shape, 1)
    sends = []
    for p in range(MAXP):
        copies[p].wait()

        @pl.when(length // PAGE == p)
        def _():
            put_row(pages, p, length % PAGE, fresh)

        for j in range(p * pieces // MAXP, (p + 1) * pieces // MAXP):
            last = (j + 1) * rows - 1 - p * PAGE
            start = last // 16 * 16
            block = pages[p, start : start + 16, :LANES].astype(jnp.float32)
            at = jnp.logical_and(row_in == last - start, lane == j)
            taken = taken + jnp.where(at, block, 0.0)
            pages[p, start : start + 16, :LANES] = jnp.where(at, ticket, block).astype(pages.dtype)
        sends.append(pltpu.make_async_copy(pages.at[p], send_ref.at[p], send_sems.at[p]))
        sends[p].start()
    taken_ref[...] = jnp.sum(taken, axis=0, keepdims=True)
    for send in sends:
        send.wait()


def pack(mesh_shape, leave_slot, target_rep, tp_index, page_table, req_lengths, qkv_new, kv_pool):
    cols = kv_pool.shape[2]
    pieces = mesh_shape[0]
    assert pieces % MAXP == 0 and pieces <= LANES
    return pl.pallas_call(
        functools.partial(pack_kernel, mesh_shape),
        out_shape=(
            pltpu.HBM((MAXP, PAGE, cols), kv_pool.dtype),
            jax.ShapeDtypeStruct((1, LANES), jnp.float32),
        ),
        in_specs=[SMEM] * 3 + [HBM] * 4,
        out_specs=(HBM, VMEM),
        scratch_shapes=[
            pltpu.SMEM(page_table.shape, page_table.dtype),
            pltpu.SMEM(req_lengths.shape, req_lengths.dtype),
            pltpu.VMEM(qkv_new.shape, qkv_new.dtype),
            pltpu.VMEM((MAXP, PAGE, cols), kv_pool.dtype),
            pltpu.SemaphoreType.DMA((3,)),
            pltpu.SemaphoreType.DMA((MAXP,)),
            pltpu.SemaphoreType.DMA((MAXP,)),
        ],
        compiler_params=params(),
        name="pack",
    )(leave_slot, target_rep, tp_index, *map(in_hbm, (page_table, req_lengths, qkv_new, kv_pool)))


def attend_kernel(
    leave_ref, table_ref, lens_ref, qkv_ref, pool_ref, proj_hbm, head_ref, new_ref, note_ref,
    stage, proj_ref, sems, proj_sem,
):
    proj_read = pltpu.make_async_copy(proj_hbm, proj_ref, proj_sem)
    proj_read.start()
    note = (lens_ref[leave_ref[0]] // PAGE).astype(jnp.float32)
    note_ref[...] = jnp.full(note_ref.shape, note, jnp.float32)
    num_req = qkv_ref.shape[0]
    cols = pool_ref.shape[2]
    heads = cols // LANES
    rows = -(-heads * GROUP // 16) * 16
    width = (GROUP + 2) * HD
    qkv = qkv_ref[...].astype(jnp.float32)
    fresh = fresh_of(qkv, cols)

    writes = []
    for r in range(num_req):
        length = lens_ref[r]
        stage[r] = pool_ref[table_ref[r, length // PAGE]]
        put_row(stage, r, length % PAGE, fresh[r : r + 1, :])
        write = pltpu.make_async_copy(stage.at[r], new_ref.at[r], sems.at[r])
        write.start()
        writes.append(write)

    queries = []
    for r in range(num_req):
        blocks = []
        for h in range(heads):
            block = jnp.concatenate(
                [qkv[r : r + 1, h * width + g * HD : h * width + (g + 2) * HD] for g in range(GROUP)], axis=0
            )
            lane = lax.broadcasted_iota(jnp.int32, block.shape, 1)
            block = jnp.where(lane < HD, block, 0.0)
            parts = [jnp.zeros_like(block)] * heads
            parts[h] = block
            blocks.append(jnp.concatenate(parts, axis=1))
        if rows > heads * GROUP:
            blocks.append(jnp.zeros((rows - heads * GROUP, cols), jnp.float32))
        queries.append(jnp.concatenate(blocks, axis=0))

    scores, masks = [], []
    for r in range(num_req):
        length = lens_ref[r]
        query = queries[r].astype(pool_ref.dtype)
        score = jnp.concatenate(
            [
                lax.dot_general(
                    query, pool_ref[table_ref[r, p]], (((1,), (1,)), ((), ())),
                    preferred_element_type=jnp.float32,
                )
                for p in range(MAXP)
            ],
            axis=1,
        )
        own = jnp.sum(queries[r] * fresh[r : r + 1, :], axis=1, keepdims=True)
        positions = lax.broadcasted_iota(jnp.int32, score.shape, 1)
        score = jnp.where(positions == length, own, score) * (1.0 / math.sqrt(HD))
        scores.append(jnp.where(positions <= length, score, -jnp.inf))
        masks.append(positions == length)
    score = jnp.concatenate(scores, axis=0)
    mask = jnp.concatenate(masks, axis=0)
    weights = jnp.exp(score - jnp.max(score, axis=1, keepdims=True))
    probs = (weights / jnp.sum(weights, axis=1, keepdims=True)).astype(pool_ref.dtype).astype(jnp.float32)
    own = jnp.sum(jnp.where(mask, probs, 0.0), axis=1, keepdims=True)
    probs = jnp.where(mask, 0.0, probs).astype(pool_ref.dtype)

    attn = []
    for r in range(num_req):
        out = own[r * rows : (r + 1) * rows, :] * fresh[r : r + 1, :]
        for p in range(MAXP):
            out = out + jnp.dot(
                probs[r * rows : (r + 1) * rows, p * PAGE : (p + 1) * PAGE], pool_ref[table_ref[r, p]],
                preferred_element_type=jnp.float32,
            )
        attn.append(
            jnp.concatenate(
                [
                    out[i : i + 1, i // GROUP * LANES + HD : (i // GROUP + 1) * LANES]
                    for i in range(heads * GROUP)
                ],
                axis=1,
            )
        )
    attn = jnp.concatenate(attn, axis=0).astype(proj_ref.dtype)
    proj_read.wait()
    head_ref[...] = jnp.dot(attn, proj_ref[...], preferred_element_type=jnp.float32)
    for write in writes:
        write.wait()


def attend(leave_slot, page_table, req_lengths, qkv_new, kv_pool, out_proj):
    num_req = qkv_new.shape[0]
    cols = kv_pool.shape[2]
    return pl.pallas_call(
        attend_kernel,
        out_shape=(
            jax.ShapeDtypeStruct((num_req, out_proj.shape[1]), jnp.float32),
            jax.ShapeDtypeStruct((num_req, PAGE, cols), kv_pool.dtype),
            jax.ShapeDtypeStruct((1, LANES), jnp.float32),
        ),
        in_specs=[SMEM, SMEM, SMEM, VMEM, VMEM, HBM],
        out_specs=(VMEM, HBM, VMEM),
        scratch_shapes=[
            pltpu.VMEM((num_req, PAGE, cols), kv_pool.dtype),
            pltpu.VMEM(out_proj.shape, out_proj.dtype),
            pltpu.SemaphoreType.DMA((num_req,)),
            pltpu.SemaphoreType.DMA,
        ],
        compiler_params=params(),
        cost_estimate=pl.CostEstimate(
            flops=2 * num_req * (2 * 16 * SPAN * cols + out_proj.size),
            bytes_accessed=2 * (num_req * SPAN * cols + out_proj.size),
            transcendentals=num_req * 16 * SPAN,
        ),
        name="attend",
    )(leave_slot, page_table, req_lengths, qkv_new, kv_pool, in_hbm(out_proj))


def experts_kernel(
    index_ref, ids_ref, gates_ref, resid_ref, gain_ref, in_ref, down_ref, *parts_refs
):
    *parts_refs, stream_ref, total_ref = parts_refs
    head = parts_refs[0][...]
    for part in parts_refs[1:]:
        head = head + part[...]
    stream = resid_ref[...].astype(jnp.float32) + head
    stream_ref[...] = stream
    mean_sq = jnp.mean(stream * stream, axis=1, keepdims=True)
    normed = (stream * lax.rsqrt(mean_sq + 1e-05) * gain_ref[...]).astype(in_ref.dtype)
    both = jnp.dot(normed, in_ref[0], preferred_element_type=jnp.float32)
    gate = both[:, :FF]
    acted = (gate / (1.0 + jnp.exp(-gate)) * both[:, FF:]).astype(down_ref.dtype)
    chosen = ids_ref[...] == index_ref[0]
    route = jnp.sum(
        jnp.where(chosen, gates_ref[...].astype(jnp.float32), 0.0), axis=1, keepdims=True
    )
    total_ref[...] = route * jnp.dot(acted, down_ref[0], preferred_element_type=jnp.float32)


def experts(tp_index, expert_ids, gate_weights, resid, norm_gain, expert_in, expert_down, parts):
    shape = jax.ShapeDtypeStruct(resid.shape, jnp.float32)
    return pl.pallas_call(
        experts_kernel,
        out_shape=(shape, shape),
        in_specs=[SMEM] + [VMEM] * (6 + len(parts)),
        out_specs=(VMEM, VMEM),
        compiler_params=params(),
        cost_estimate=pl.CostEstimate(
            flops=2 * resid.shape[0] * (expert_in.size + expert_down.size),
            bytes_accessed=2 * (expert_in.size + expert_down.size),
            transcendentals=resid.shape[0] * FF,
        ),
        name="experts",
    )(
        tp_index, expert_ids, gate_weights, resid, norm_gain[None, :], expert_in, expert_down, *parts
    )


def forward_kernel(
    mesh_shape, leave_ref, target_ref, tp_ref, index_ref, landed_ref, hidden_ref, note_ref, taken_ref, send_ref
):
    pieces, rows, cols = landed_ref.shape
    body = rows * cols // LANES
    send_ref[:, body:, :] = jnp.zeros((pieces, EXTRA, LANES), send_ref.dtype)
    own = place_of(index_ref[0], tp_ref[0], mesh_shape)
    lane = lax.broadcasted_iota(jnp.int32, (1, LANES), 1)
    for s in range(pieces):
        last = landed_ref[s, rows - 1 :, :LANES].astype(jnp.float32)
        place = jnp.max(jnp.where(lane == own, last, 0.0)).astype(jnp.int32)
        for c in range(cols // LANES):
            send_ref[place, c * rows : (c + 1) * rows, :] = landed_ref[s, :, c * LANES : (c + 1) * LANES]
    hidden = hidden_ref[...].astype(jnp.float32)
    at_row = lax.broadcasted_iota(jnp.int32, hidden.shape, 0) == leave_ref[0]
    row = jnp.sum(jnp.where(at_row, hidden, 0.0), axis=0, keepdims=True)
    spare = (EXTRA - 2) * LANES - row.shape[1]
    if spare:
        row = jnp.concatenate([row, jnp.zeros((1, spare), jnp.float32)], axis=1)
    lines = [row[:, k * LANES : (k + 1) * LANES] for k in range(EXTRA - 2)]
    place = place_of(target_ref[0], tp_ref[0], mesh_shape)
    extra = jnp.concatenate(lines + [taken_ref[...], note_ref[...]], axis=0)
    send_ref[place, body:, :] = extra.astype(send_ref.dtype)


def forward(mesh_shape, leave_slot, target_rep, tp_index, rep_index, landed, hidden, note, taken):
    pieces, rows, cols = landed.shape
    return pl.pallas_call(
        functools.partial(forward_kernel, mesh_shape),
        out_shape=jax.ShapeDtypeStruct((pieces, rows * cols // LANES + EXTRA, LANES), landed.dtype),
        in_specs=[SMEM] * 4 + [VMEM] * 4,
        out_specs=VMEM,
        compiler_params=params(),
        name="forward",
    )(leave_slot, target_rep, tp_index, rep_index, landed, hidden, note, taken)


def settle_kernel(
    leave_ref, landed_ref, hidden_ref, new_in_ref, hidden_out_ref, new_ref, arrived_ref,
    pages, mixed, page_sems, new_sem, hidden_sem,
):
    del new_in_ref
    pieces, slot_rows, _ = landed_ref.shape
    body = slot_rows - EXTRA
    cols = pages.shape[2]
    rows = SPAN // pieces
    leave = leave_ref[0]
    extra = jnp.sum(landed_ref[:, body:, :].astype(jnp.float32), axis=0)
    taken = extra[EXTRA - 2 : EXTRA - 1, :]
    row_in = lax.broadcasted_iota(jnp.int32, (rows, LANES), 0)
    lane = lax.broadcasted_iota(jnp.int32, (rows, LANES), 1)
    writes = []
    for p in range(MAXP):
        for j in range(p * pieces // MAXP, (p + 1) * pieces // MAXP):
            start = j * rows - p * PAGE
            for c in range(cols // LANES):
                block = landed_ref[j, c * rows : (c + 1) * rows, :]
                if c == 0:
                    at = jnp.logical_and(row_in == rows - 1, lane == j)
                    block = jnp.where(at, taken, block.astype(jnp.float32)).astype(pages.dtype)
                pages[p, start : start + rows, c * LANES : (c + 1) * LANES] = block
        writes.append(pltpu.make_async_copy(pages.at[p], arrived_ref.at[p], page_sems.at[p]))
        writes[p].start()
    page = jnp.max(extra[EXTRA - 1 :, :]).astype(jnp.int32)
    writes.append(pltpu.make_async_copy(pages.at[page], new_ref.at[leave], new_sem))
    writes[-1].start()
    width = hidden_ref.shape[1]
    row = jnp.concatenate([extra[k : k + 1, :] for k in range(-(-width // LANES))], axis=1)
    hidden = hidden_ref[...].astype(jnp.float32)
    at_row = lax.broadcasted_iota(jnp.int32, hidden.shape, 0) == leave
    mixed[...] = jnp.where(at_row, row[:, :width], hidden).astype(mixed.dtype)
    writes.append(pltpu.make_async_copy(mixed, hidden_out_ref, hidden_sem))
    writes[-1].start()
    for write in writes:
        write.wait()


def settle(leave_slot, landed, hidden, new_pages):
    arrived = (MAXP,) + new_pages.shape[1:]
    return pl.pallas_call(
        settle_kernel,
        out_shape=(
            jax.ShapeDtypeStruct(hidden.shape, hidden.dtype),
            jax.ShapeDtypeStruct(new_pages.shape, new_pages.dtype),
            jax.ShapeDtypeStruct(arrived, new_pages.dtype),
        ),
        in_specs=[SMEM, VMEM, VMEM, HBM],
        out_specs=(HBM, HBM, HBM),
        scratch_shapes=[
            pltpu.VMEM(arrived, new_pages.dtype),
            pltpu.VMEM(hidden.shape, hidden.dtype),
            pltpu.SemaphoreType.DMA((MAXP,)),
            pltpu.SemaphoreType.DMA,
            pltpu.SemaphoreType.DMA,
        ],
        input_output_aliases={3: 1},
        compiler_params=params(),
        name="settle",
    )(leave_slot, landed, hidden, new_pages)


def local(
    kv_pool,
    page_table,
    req_lengths,
    leave_slot,
    target_rep,
    qkv_new,
    residual_in,
    expert_ids,
    gate_weights,
    norm_gain,
    out_proj,
    expert_in,
    expert_down,
):
    pieces, tp_size = mesh_shape = lax.axis_size("rep"), lax.axis_size("tp")
    rep_index, tp_index = lax.axis_index("rep")[None], lax.axis_index("tp")[None]
    orders = ORDERS.get(mesh_shape, (tuple(range(pieces)),) * tp_size)
    groups = [[peer * tp_size + core for peer in peers] for core, peers in enumerate(orders)]

    def exchange(packet):
        return lax.all_to_all(
            packet, ("rep", "tp"), split_axis=0, concat_axis=0, tiled=True, axis_index_groups=groups
        )

    send, taken = pack(
        mesh_shape, leave_slot, target_rep, tp_index, page_table, req_lengths, qkv_new, kv_pool
    )
    send, qkv_new = lax.optimization_barrier((send, qkv_new))
    landed = exchange(send.reshape(pieces, SPAN // pieces, kv_pool.shape[2]))

    head_part, new_pages, note = attend(
        leave_slot, page_table, req_lengths, qkv_new, kv_pool, out_proj
    )
    shifts = [[(i, (i + k) % tp_size) for i in range(tp_size)] for k in range(1, tp_size)]
    parts = [head_part] + [lax.ppermute(head_part, "tp", shift) for shift in shifts]
    assert expert_in.shape[0] == 1
    stream, total = experts(
        tp_index, expert_ids, gate_weights, residual_in, norm_gain, expert_in, expert_down, parts
    )
    width = stream.shape[1] // tp_size

    def share(values, index):
        return lax.dynamic_slice_in_dim(values, index * width, width, 1)

    mix = share(total, tp_index[0])
    for k, shift in enumerate(shifts, 1):
        mix = mix + lax.ppermute(share(total, (tp_index[0] + k) % tp_size), "tp", shift)
    hidden = (share(stream, tp_index[0]) + mix).astype(jnp.bfloat16)
    landed = exchange(
        forward(mesh_shape, leave_slot, target_rep, tp_index, rep_index, landed, hidden, note, taken)
    )
    return settle(leave_slot, landed, hidden, new_pages)


def solution(mesh):
    return jax.shard_map(
        local,
        mesh=mesh,
        in_specs=(
            P("rep", None, "tp"),
            P("rep", None),
            P("rep"),
            P("rep"),
            P("rep"),
            P("rep", "tp"),
            P("rep", None),
            P("rep", None),
            P("rep", None),
            P(),
            P("tp", None),
            P("tp", None, None),
            P("tp", None, None),
        ),
        out_specs=(P("rep", "tp"), P("rep", None, "tp"), P("rep", None, "tp")),
        check_vma=False,
    )
```

```python
import functools
import math

import jax
import jax.numpy as jnp
from jax import lax
from jax.experimental import pallas as pl
from jax.experimental.pallas import tpu as pltpu
from jax.sharding import PartitionSpec as P

QH = 24
KVH = 8
HD = 64
FF = 256
PAGE = 128
MAXP = 4
GROUP = QH // KVH
SPAN = MAXP * PAGE
LANES = 128
EXTRA = 8
VMEM_BYTES = 16 * 1024 * 1024
SPREAD = {(16, 2): (
    (0, 8, 2, 3, 4, 5, 6, 13, 1, 15, 10, 11, 14, 7, 12, 9),
    (10, 9, 8, 11, 4, 15, 12, 0, 2, 3, 1, 13, 14, 7, 6, 5),
)}
DELIVER = {(16, 2): (
    (3, 8, 2, 0, 4, 5, 6, 13, 1, 15, 10, 11, 14, 7, 12, 9),
    (10, 9, 12, 11, 4, 15, 8, 6, 2, 3, 5, 13, 14, 7, 0, 1),
)}

SMEM = pl.BlockSpec(memory_space=pltpu.SMEM)
VMEM = pl.BlockSpec(memory_space=pltpu.VMEM)
HBM = pl.BlockSpec(memory_space=pltpu.HBM)


def in_hbm(array):
    return pltpu.with_memory_space_constraint(array, pltpu.HBM)


def params():
    return pltpu.CompilerParams(vmem_limit_bytes=VMEM_BYTES)


def place_of(replica, tp_index, orders):
    place = replica
    for core, peers in enumerate(orders):
        for k, peer in enumerate(peers):
            hit = jnp.logical_and(replica == peer, tp_index == core)
            place = jnp.where(hit, k, place)
    return place


def fresh_of(qkv, cols):
    width = (GROUP + 2) * HD
    return jnp.concatenate(
        [qkv[:, h * width + GROUP * HD : (h + 1) * width] for h in range(cols // LANES)], axis=1
    )


def put_row(ref, lead, row, fresh):
    start = pl.multiple_of(row // 16 * 16, 16)
    block = ref[lead, pl.ds(start, 16), :].astype(jnp.float32)
    at_row = lax.broadcasted_iota(jnp.int32, block.shape, 0) == row - start
    ref[lead, pl.ds(start, 16), :] = jnp.where(at_row, fresh, block).astype(ref.dtype)


def pack_kernel(
    mesh_shape, leave_ref, target_ref, tp_ref, table_hbm, lens_hbm, qkv_hbm, pool_ref, send_ref, taken_ref,
    table_ref, lens_ref, qkv_ref, pages, small_sems, page_sems, send_sems,
):
    smalls = [
        pltpu.make_async_copy(source, target, small_sems.at[i])
        for i, (source, target) in enumerate(
            [(table_hbm, table_ref), (lens_hbm, lens_ref), (qkv_hbm, qkv_ref)]
        )
    ]
    for copy in smalls:
        copy.start()
    smalls[0].wait()
    leave = leave_ref[0]
    copies = [
        pltpu.make_async_copy(pool_ref.at[table_ref[leave, p]], pages.at[p], page_sems.at[p])
        for p in range(MAXP)
    ]
    for copy in copies:
        copy.start()
    cols = pages.shape[2]
    pieces = mesh_shape[0]
    rows = SPAN // pieces
    ticket = place_of(target_ref[0], tp_ref[0], DELIVER.get(mesh_shape, ())).astype(jnp.float32)
    smalls[1].wait()
    smalls[2].wait()
    qkv = qkv_ref[...].astype(jnp.float32)
    at_row = lax.broadcasted_iota(jnp.int32, qkv.shape, 0) == leave
    qkv = jnp.sum(jnp.where(at_row, qkv, 0.0), axis=0, keepdims=True)
    fresh = fresh_of(qkv, cols)
    length = lens_ref[leave]
    taken = jnp.zeros((16, LANES), jnp.float32)
    row_in = lax.broadcasted_iota(jnp.int32, taken.shape, 0)
    lane = lax.broadcasted_iota(jnp.int32, taken.shape, 1)
    sends = []
    for p in range(MAXP):
        copies[p].wait()

        @pl.when(length // PAGE == p)
        def _():
            put_row(pages, p, length % PAGE, fresh)

        for j in range(p * pieces // MAXP, (p + 1) * pieces // MAXP):
            last = (j + 1) * rows - 1 - p * PAGE
            start = last // 16 * 16
            block = pages[p, start : start + 16, :LANES].astype(jnp.float32)
            at = jnp.logical_and(row_in == last - start, lane == j)
            taken = taken + jnp.where(at, block, 0.0)
            pages[p, start : start + 16, :LANES] = jnp.where(at, ticket, block).astype(pages.dtype)
        sends.append(pltpu.make_async_copy(pages.at[p], send_ref.at[p], send_sems.at[p]))
        sends[p].start()
    taken_ref[...] = jnp.sum(taken, axis=0, keepdims=True)
    for send in sends:
        send.wait()


def pack(mesh_shape, leave_slot, target_rep, tp_index, page_table, req_lengths, qkv_new, kv_pool):
    cols = kv_pool.shape[2]
    pieces = mesh_shape[0]
    assert pieces % MAXP == 0 and pieces <= LANES
    return pl.pallas_call(
        functools.partial(pack_kernel, mesh_shape),
        out_shape=(
            pltpu.HBM((MAXP, PAGE, cols), kv_pool.dtype),
            jax.ShapeDtypeStruct((1, LANES), jnp.float32),
        ),
        in_specs=[SMEM] * 3 + [HBM] * 4,
        out_specs=(HBM, VMEM),
        scratch_shapes=[
            pltpu.SMEM(page_table.shape, page_table.dtype),
            pltpu.SMEM(req_lengths.shape, req_lengths.dtype),
            pltpu.VMEM(qkv_new.shape, qkv_new.dtype),
            pltpu.VMEM((MAXP, PAGE, cols), kv_pool.dtype),
            pltpu.SemaphoreType.DMA((3,)),
            pltpu.SemaphoreType.DMA((MAXP,)),
            pltpu.SemaphoreType.DMA((MAXP,)),
        ],
        compiler_params=params(),
        name="pack",
    )(leave_slot, target_rep, tp_index, *map(in_hbm, (page_table, req_lengths, qkv_new, kv_pool)))


def attend_kernel(
    leave_ref, table_ref, lens_ref, qkv_ref, pool_ref, proj_hbm, head_ref, new_ref, note_ref,
    stage, proj_ref, sems, proj_sem,
):
    proj_read = pltpu.make_async_copy(proj_hbm, proj_ref, proj_sem)
    proj_read.start()
    note = (lens_ref[leave_ref[0]] // PAGE).astype(jnp.float32)
    note_ref[...] = jnp.full(note_ref.shape, note, jnp.float32)
    num_req = qkv_ref.shape[0]
    cols = pool_ref.shape[2]
    heads = cols // LANES
    rows = -(-heads * GROUP // 16) * 16
    width = (GROUP + 2) * HD
    qkv = qkv_ref[...].astype(jnp.float32)
    fresh = fresh_of(qkv, cols)

    writes = []
    for r in range(num_req):
        length = lens_ref[r]
        stage[r] = pool_ref[table_ref[r, length // PAGE]]
        put_row(stage, r, length % PAGE, fresh[r : r + 1, :])
        write = pltpu.make_async_copy(stage.at[r], new_ref.at[r], sems.at[r])
        write.start()
        writes.append(write)

    queries = []
    for r in range(num_req):
        blocks = []
        for h in range(heads):
            block = jnp.concatenate(
                [qkv[r : r + 1, h * width + g * HD : h * width + (g + 2) * HD] for g in range(GROUP)], axis=0
            )
            lane = lax.broadcasted_iota(jnp.int32, block.shape, 1)
            block = jnp.where(lane < HD, block, 0.0)
            parts = [jnp.zeros_like(block)] * heads
            parts[h] = block
            blocks.append(jnp.concatenate(parts, axis=1))
        if rows > heads * GROUP:
            blocks.append(jnp.zeros((rows - heads * GROUP, cols), jnp.float32))
        queries.append(jnp.concatenate(blocks, axis=0))

    scores, masks = [], []
    for r in range(num_req):
        length = lens_ref[r]
        query = queries[r].astype(pool_ref.dtype)
        score = jnp.concatenate(
            [
                lax.dot_general(
                    query, pool_ref[table_ref[r, p]], (((1,), (1,)), ((), ())),
                    preferred_element_type=jnp.float32,
                )
                for p in range(MAXP)
            ],
            axis=1,
        )
        own = jnp.sum(queries[r] * fresh[r : r + 1, :], axis=1, keepdims=True)
        positions = lax.broadcasted_iota(jnp.int32, score.shape, 1)
        score = jnp.where(positions == length, own, score) * (1.0 / math.sqrt(HD))
        scores.append(jnp.where(positions <= length, score, -jnp.inf))
        masks.append(positions == length)
    score = jnp.concatenate(scores, axis=0)
    mask = jnp.concatenate(masks, axis=0)
    weights = jnp.exp(score - jnp.max(score, axis=1, keepdims=True))
    probs = (weights / jnp.sum(weights, axis=1, keepdims=True)).astype(pool_ref.dtype).astype(jnp.float32)
    own = jnp.sum(jnp.where(mask, probs, 0.0), axis=1, keepdims=True)
    probs = jnp.where(mask, 0.0, probs).astype(pool_ref.dtype)

    attn = []
    for r in range(num_req):
        out = own[r * rows : (r + 1) * rows, :] * fresh[r : r + 1, :]
        for p in range(MAXP):
            out = out + jnp.dot(
                probs[r * rows : (r + 1) * rows, p * PAGE : (p + 1) * PAGE], pool_ref[table_ref[r, p]],
                preferred_element_type=jnp.float32,
            )
        attn.append(
            jnp.concatenate(
                [
                    out[i : i + 1, i // GROUP * LANES + HD : (i // GROUP + 1) * LANES]
                    for i in range(heads * GROUP)
                ],
                axis=1,
            )
        )
    attn = jnp.concatenate(attn, axis=0).astype(proj_ref.dtype)
    proj_read.wait()
    head_ref[...] = jnp.dot(attn, proj_ref[...], preferred_element_type=jnp.float32)
    for write in writes:
        write.wait()


def attend(leave_slot, page_table, req_lengths, qkv_new, kv_pool, out_proj):
    num_req = qkv_new.shape[0]
    cols = kv_pool.shape[2]
    return pl.pallas_call(
        attend_kernel,
        out_shape=(
            jax.ShapeDtypeStruct((num_req, out_proj.shape[1]), jnp.float32),
            jax.ShapeDtypeStruct((num_req, PAGE, cols), kv_pool.dtype),
            jax.ShapeDtypeStruct((1, LANES), jnp.float32),
        ),
        in_specs=[SMEM, SMEM, SMEM, VMEM, VMEM, HBM],
        out_specs=(VMEM, HBM, VMEM),
        scratch_shapes=[
            pltpu.VMEM((num_req, PAGE, cols), kv_pool.dtype),
            pltpu.VMEM(out_proj.shape, out_proj.dtype),
            pltpu.SemaphoreType.DMA((num_req,)),
            pltpu.SemaphoreType.DMA,
        ],
        compiler_params=params(),
        cost_estimate=pl.CostEstimate(
            flops=2 * num_req * (2 * 16 * SPAN * cols + out_proj.size),
            bytes_accessed=2 * (num_req * SPAN * cols + out_proj.size),
            transcendentals=num_req * 16 * SPAN,
        ),
        name="attend",
    )(leave_slot, page_table, req_lengths, qkv_new, kv_pool, in_hbm(out_proj))


def experts_kernel(
    index_ref, ids_ref, gates_ref, resid_ref, gain_ref, in_ref, down_ref, *parts_refs
):
    *parts_refs, stream_ref, total_ref = parts_refs
    head = parts_refs[0][...]
    for part in parts_refs[1:]:
        head = head + part[...]
    stream = resid_ref[...].astype(jnp.float32) + head
    stream_ref[...] = stream
    mean_sq = jnp.mean(stream * stream, axis=1, keepdims=True)
    normed = (stream * lax.rsqrt(mean_sq + 1e-05) * gain_ref[...]).astype(in_ref.dtype)
    both = jnp.dot(normed, in_ref[0], preferred_element_type=jnp.float32)
    gate = both[:, :FF]
    acted = (gate / (1.0 + jnp.exp(-gate)) * both[:, FF:]).astype(down_ref.dtype)
    chosen = ids_ref[...] == index_ref[0]
    route = jnp.sum(
        jnp.where(chosen, gates_ref[...].astype(jnp.float32), 0.0), axis=1, keepdims=True
    )
    total_ref[...] = route * jnp.dot(acted, down_ref[0], preferred_element_type=jnp.float32)


def experts(tp_index, expert_ids, gate_weights, resid, norm_gain, expert_in, expert_down, parts):
    shape = jax.ShapeDtypeStruct(resid.shape, jnp.float32)
    return pl.pallas_call(
        experts_kernel,
        out_shape=(shape, shape),
        in_specs=[SMEM] + [VMEM] * (6 + len(parts)),
        out_specs=(VMEM, VMEM),
        compiler_params=params(),
        cost_estimate=pl.CostEstimate(
            flops=2 * resid.shape[0] * (expert_in.size + expert_down.size),
            bytes_accessed=2 * (expert_in.size + expert_down.size),
            transcendentals=resid.shape[0] * FF,
        ),
        name="experts",
    )(
        tp_index, expert_ids, gate_weights, resid, norm_gain[None, :], expert_in, expert_down, *parts
    )


def forward_kernel(
    mesh_shape, leave_ref, target_ref, tp_ref, index_ref, landed_ref, hidden_ref, note_ref, taken_ref, send_ref
):
    pieces, rows, cols = landed_ref.shape
    body = rows * cols // LANES
    send_ref[:, body:, :] = jnp.zeros((pieces, EXTRA, LANES), send_ref.dtype)
    own = place_of(index_ref[0], tp_ref[0], SPREAD.get(mesh_shape, ()))
    lane = lax.broadcasted_iota(jnp.int32, (1, LANES), 1)
    for s in range(pieces):
        last = landed_ref[s, rows - 1 :, :LANES].astype(jnp.float32)
        place = jnp.max(jnp.where(lane == own, last, 0.0)).astype(jnp.int32)
        for c in range(cols // LANES):
            send_ref[place, c * rows : (c + 1) * rows, :] = landed_ref[s, :, c * LANES : (c + 1) * LANES]
    hidden = hidden_ref[...].astype(jnp.float32)
    at_row = lax.broadcasted_iota(jnp.int32, hidden.shape, 0) == leave_ref[0]
    row = jnp.sum(jnp.where(at_row, hidden, 0.0), axis=0, keepdims=True)
    spare = (EXTRA - 2) * LANES - row.shape[1]
    if spare:
        row = jnp.concatenate([row, jnp.zeros((1, spare), jnp.float32)], axis=1)
    lines = [row[:, k * LANES : (k + 1) * LANES] for k in range(EXTRA - 2)]
    place = place_of(target_ref[0], tp_ref[0], DELIVER.get(mesh_shape, ()))
    extra = jnp.concatenate(lines + [taken_ref[...], note_ref[...]], axis=0)
    send_ref[place, body:, :] = extra.astype(send_ref.dtype)


def forward(mesh_shape, leave_slot, target_rep, tp_index, rep_index, landed, hidden, note, taken):
    pieces, rows, cols = landed.shape
    return pl.pallas_call(
        functools.partial(forward_kernel, mesh_shape),
        out_shape=jax.ShapeDtypeStruct((pieces, rows * cols // LANES + EXTRA, LANES), landed.dtype),
        in_specs=[SMEM] * 4 + [VMEM] * 4,
        out_specs=VMEM,
        compiler_params=params(),
        name="forward",
    )(leave_slot, target_rep, tp_index, rep_index, landed, hidden, note, taken)


def settle_kernel(
    mesh_shape, leave_ref, tp_ref, landed_ref, hidden_ref, new_in_ref, hidden_out_ref, new_ref, arrived_ref,
    pages, mixed, page_sems, new_sem, hidden_sem,
):
    del new_in_ref
    pieces, slot_rows, _ = landed_ref.shape
    body = slot_rows - EXTRA
    cols = pages.shape[2]
    rows = SPAN // pieces
    leave = leave_ref[0]
    orders = list(zip(SPREAD.get(mesh_shape, ()), DELIVER.get(mesh_shape, ())))
    extra = jnp.sum(landed_ref[:, body:, :].astype(jnp.float32), axis=0)
    taken = extra[EXTRA - 2 : EXTRA - 1, :]
    row_in = lax.broadcasted_iota(jnp.int32, (rows, LANES), 0)
    lane = lax.broadcasted_iota(jnp.int32, (rows, LANES), 1)
    writes = []
    for p in range(MAXP):
        for j in range(p * pieces // MAXP, (p + 1) * pieces // MAXP):
            start = j * rows - p * PAGE
            slot = j
            for core, (spread, deliver) in enumerate(orders):
                slot = jnp.where(tp_ref[0] == core, deliver.index(spread[j]), slot)
            for c in range(cols // LANES):
                block = landed_ref[slot, c * rows : (c + 1) * rows, :]
                if c == 0:
                    at = jnp.logical_and(row_in == rows - 1, lane == j)
                    block = jnp.where(at, taken, block.astype(jnp.float32)).astype(pages.dtype)
                pages[p, start : start + rows, c * LANES : (c + 1) * LANES] = block
        writes.append(pltpu.make_async_copy(pages.at[p], arrived_ref.at[p], page_sems.at[p]))
        writes[p].start()
    page = jnp.max(extra[EXTRA - 1 :, :]).astype(jnp.int32)
    writes.append(pltpu.make_async_copy(pages.at[page], new_ref.at[leave], new_sem))
    writes[-1].start()
    width = hidden_ref.shape[1]
    row = jnp.concatenate([extra[k : k + 1, :] for k in range(-(-width // LANES))], axis=1)
    hidden = hidden_ref[...].astype(jnp.float32)
    at_row = lax.broadcasted_iota(jnp.int32, hidden.shape, 0) == leave
    mixed[...] = jnp.where(at_row, row[:, :width], hidden).astype(mixed.dtype)
    writes.append(pltpu.make_async_copy(mixed, hidden_out_ref, hidden_sem))
    writes[-1].start()
    for write in writes:
        write.wait()


def settle(mesh_shape, leave_slot, tp_index, landed, hidden, new_pages):
    arrived = (MAXP,) + new_pages.shape[1:]
    return pl.pallas_call(
        functools.partial(settle_kernel, mesh_shape),
        out_shape=(
            jax.ShapeDtypeStruct(hidden.shape, hidden.dtype),
            jax.ShapeDtypeStruct(new_pages.shape, new_pages.dtype),
            jax.ShapeDtypeStruct(arrived, new_pages.dtype),
        ),
        in_specs=[SMEM, SMEM, VMEM, VMEM, HBM],
        out_specs=(HBM, HBM, HBM),
        scratch_shapes=[
            pltpu.VMEM(arrived, new_pages.dtype),
            pltpu.VMEM(hidden.shape, hidden.dtype),
            pltpu.SemaphoreType.DMA((MAXP,)),
            pltpu.SemaphoreType.DMA,
            pltpu.SemaphoreType.DMA,
        ],
        input_output_aliases={4: 1},
        compiler_params=params(),
        name="settle",
    )(leave_slot, tp_index, landed, hidden, new_pages)


def local(
    kv_pool,
    page_table,
    req_lengths,
    leave_slot,
    target_rep,
    qkv_new,
    residual_in,
    expert_ids,
    gate_weights,
    norm_gain,
    out_proj,
    expert_in,
    expert_down,
):
    pieces, tp_size = mesh_shape = lax.axis_size("rep"), lax.axis_size("tp")
    rep_index, tp_index = lax.axis_index("rep")[None], lax.axis_index("tp")[None]

    def exchange(packet, orders):
        orders = orders.get(mesh_shape, (tuple(range(pieces)),) * tp_size)
        groups = [[peer * tp_size + core for peer in peers] for core, peers in enumerate(orders)]
        return lax.all_to_all(
            packet, ("rep", "tp"), split_axis=0, concat_axis=0, tiled=True, axis_index_groups=groups
        )

    send, taken = pack(
        mesh_shape, leave_slot, target_rep, tp_index, page_table, req_lengths, qkv_new, kv_pool
    )
    send, qkv_new = lax.optimization_barrier((send, qkv_new))
    landed = exchange(send.reshape(pieces, SPAN // pieces, kv_pool.shape[2]), SPREAD)

    head_part, new_pages, note = attend(
        leave_slot, page_table, req_lengths, qkv_new, kv_pool, out_proj
    )
    shifts = [[(i, (i + k) % tp_size) for i in range(tp_size)] for k in range(1, tp_size)]
    parts = [head_part] + [lax.ppermute(head_part, "tp", shift) for shift in shifts]
    assert expert_in.shape[0] == 1
    stream, total = experts(
        tp_index, expert_ids, gate_weights, residual_in, norm_gain, expert_in, expert_down, parts
    )
    width = stream.shape[1] // tp_size

    def share(values, index):
        return lax.dynamic_slice_in_dim(values, index * width, width, 1)

    mix = share(total, tp_index[0])
    for k, shift in enumerate(shifts, 1):
        mix = mix + lax.ppermute(share(total, (tp_index[0] + k) % tp_size), "tp", shift)
    hidden = (share(stream, tp_index[0]) + mix).astype(jnp.bfloat16)
    landed = exchange(
        forward(mesh_shape, leave_slot, target_rep, tp_index, rep_index, landed, hidden, note, taken),
        DELIVER,
    )
    return settle(mesh_shape, leave_slot, tp_index, landed, hidden, new_pages)


def solution(mesh):
    return jax.shard_map(
        local,
        mesh=mesh,
        in_specs=(
            P("rep", None, "tp"),
            P("rep", None),
            P("rep"),
            P("rep"),
            P("rep"),
            P("rep", "tp"),
            P("rep", None),
            P("rep", None),
            P("rep", None),
            P(),
            P("tp", None),
            P("tp", None, None),
            P("tp", None, None),
        ),
        out_specs=(P("rep", "tp"), P("rep", None, "tp"), P("rep", None, "tp")),
        check_vma=False,
    )
```

```python
import functools
import math

import jax
import jax.numpy as jnp
from jax import lax
from jax.experimental import pallas as pl
from jax.experimental.pallas import tpu as pltpu
from jax.sharding import PartitionSpec as P

QH = 24
KVH = 8
HD = 64
FF = 256
PAGE = 128
MAXP = 4
GROUP = QH // KVH
SPAN = MAXP * PAGE
LANES = 128
EXTRA = 8
VMEM_BYTES = 16 * 1024 * 1024
SPREAD = {(16, 2): (
    (0, 8, 2, 3, 4, 5, 6, 13, 1, 15, 10, 11, 14, 7, 12, 9),
    (10, 9, 8, 11, 4, 15, 12, 0, 2, 3, 1, 13, 14, 7, 6, 5),
)}
DELIVER = {(16, 2): (
    (3, 8, 2, 0, 4, 5, 6, 13, 1, 15, 10, 11, 14, 7, 12, 9),
    (10, 9, 12, 11, 4, 15, 8, 6, 2, 3, 5, 13, 14, 7, 0, 1),
)}

SMEM = pl.BlockSpec(memory_space=pltpu.SMEM)
VMEM = pl.BlockSpec(memory_space=pltpu.VMEM)
HBM = pl.BlockSpec(memory_space=pltpu.HBM)


def in_hbm(array):
    return pltpu.with_memory_space_constraint(array, pltpu.HBM)


def params():
    return pltpu.CompilerParams(vmem_limit_bytes=VMEM_BYTES)


def place_of(replica, tp_index, orders):
    place = replica
    for core, peers in enumerate(orders):
        for k, peer in enumerate(peers):
            hit = jnp.logical_and(replica == peer, tp_index == core)
            place = jnp.where(hit, k, place)
    return place


def fresh_of(qkv, cols):
    width = (GROUP + 2) * HD
    return jnp.concatenate(
        [qkv[:, h * width + GROUP * HD : (h + 1) * width] for h in range(cols // LANES)], axis=1
    )


def put_row(ref, lead, row, fresh):
    start = pl.multiple_of(row // 16 * 16, 16)
    block = ref[lead, pl.ds(start, 16), :].astype(jnp.float32)
    at_row = lax.broadcasted_iota(jnp.int32, block.shape, 0) == row - start
    ref[lead, pl.ds(start, 16), :] = jnp.where(at_row, fresh, block).astype(ref.dtype)


def pack_kernel(
    mesh_shape, leave_ref, target_ref, tp_ref, table_hbm, lens_hbm, qkv_hbm, pool_ref, send_ref, taken_ref,
    table_ref, lens_ref, qkv_ref, pages, small_sems, page_sems, send_sems,
):
    smalls = [
        pltpu.make_async_copy(source, target, small_sems.at[i])
        for i, (source, target) in enumerate(
            [(table_hbm, table_ref), (lens_hbm, lens_ref), (qkv_hbm, qkv_ref)]
        )
    ]
    for copy in smalls:
        copy.start()
    smalls[0].wait()
    leave = leave_ref[0]
    copies = [
        pltpu.make_async_copy(pool_ref.at[table_ref[leave, p]], pages.at[p], page_sems.at[p])
        for p in range(MAXP)
    ]
    for copy in copies:
        copy.start()
    cols = pages.shape[2]
    pieces = mesh_shape[0]
    rows = SPAN // pieces
    ticket = place_of(target_ref[0], tp_ref[0], DELIVER.get(mesh_shape, ())).astype(jnp.float32)
    smalls[1].wait()
    smalls[2].wait()
    qkv = qkv_ref[...].astype(jnp.float32)
    at_row = lax.broadcasted_iota(jnp.int32, qkv.shape, 0) == leave
    qkv = jnp.sum(jnp.where(at_row, qkv, 0.0), axis=0, keepdims=True)
    fresh = fresh_of(qkv, cols)
    length = lens_ref[leave]
    taken = jnp.zeros((16, LANES), jnp.float32)
    row_in = lax.broadcasted_iota(jnp.int32, taken.shape, 0)
    lane = lax.broadcasted_iota(jnp.int32, taken.shape, 1)
    sends = []
    for p in range(MAXP):
        copies[p].wait()

        @pl.when(length // PAGE == p)
        def _():
            put_row(pages, p, length % PAGE, fresh)

        for j in range(p * pieces // MAXP, (p + 1) * pieces // MAXP):
            last = (j + 1) * rows - 1 - p * PAGE
            start = last // 16 * 16
            block = pages[p, start : start + 16, :LANES].astype(jnp.float32)
            at = jnp.logical_and(row_in == last - start, lane == j)
            taken = taken + jnp.where(at, block, 0.0)
            pages[p, start : start + 16, :LANES] = jnp.where(at, ticket, block).astype(pages.dtype)
        sends.append(pltpu.make_async_copy(pages.at[p], send_ref.at[p], send_sems.at[p]))
        sends[p].start()
    taken_ref[...] = jnp.sum(taken, axis=0, keepdims=True)
    for send in sends:
        send.wait()


def pack(mesh_shape, leave_slot, target_rep, tp_index, page_table, req_lengths, qkv_new, kv_pool):
    cols = kv_pool.shape[2]
    pieces = mesh_shape[0]
    assert pieces % MAXP == 0 and pieces <= LANES
    return pl.pallas_call(
        functools.partial(pack_kernel, mesh_shape),
        out_shape=(
            pltpu.HBM((MAXP, PAGE, cols), kv_pool.dtype),
            jax.ShapeDtypeStruct((1, LANES), jnp.float32),
        ),
        in_specs=[SMEM] * 3 + [HBM] * 4,
        out_specs=(HBM, VMEM),
        scratch_shapes=[
            pltpu.SMEM(page_table.shape, page_table.dtype),
            pltpu.SMEM(req_lengths.shape, req_lengths.dtype),
            pltpu.VMEM(qkv_new.shape, qkv_new.dtype),
            pltpu.VMEM((MAXP, PAGE, cols), kv_pool.dtype),
            pltpu.SemaphoreType.DMA((3,)),
            pltpu.SemaphoreType.DMA((MAXP,)),
            pltpu.SemaphoreType.DMA((MAXP,)),
        ],
        compiler_params=params(),
        name="pack",
    )(leave_slot, target_rep, tp_index, *map(in_hbm, (page_table, req_lengths, qkv_new, kv_pool)))


def attend_kernel(
    leave_ref, table_ref, lens_ref, qkv_ref, pool_ref, proj_hbm, head_ref, new_ref, note_ref,
    stage, proj_ref, sems, proj_sem,
):
    proj_read = pltpu.make_async_copy(proj_hbm, proj_ref, proj_sem)
    proj_read.start()
    note = (lens_ref[leave_ref[0]] // PAGE).astype(jnp.float32)
    note_ref[...] = jnp.full(note_ref.shape, note, jnp.float32)
    num_req = qkv_ref.shape[0]
    cols = pool_ref.shape[2]
    heads = cols // LANES
    rows = -(-heads * GROUP // 16) * 16
    width = (GROUP + 2) * HD
    qkv = qkv_ref[...].astype(jnp.float32)
    fresh = fresh_of(qkv, cols)

    writes = []
    for r in range(num_req):
        length = lens_ref[r]
        stage[r] = pool_ref[table_ref[r, length // PAGE]]
        put_row(stage, r, length % PAGE, fresh[r : r + 1, :])
        write = pltpu.make_async_copy(stage.at[r], new_ref.at[r], sems.at[r])
        write.start()
        writes.append(write)

    queries = []
    for r in range(num_req):
        blocks = []
        for h in range(heads):
            block = jnp.concatenate(
                [qkv[r : r + 1, h * width + g * HD : h * width + (g + 2) * HD] for g in range(GROUP)], axis=0
            )
            lane = lax.broadcasted_iota(jnp.int32, block.shape, 1)
            block = jnp.where(lane < HD, block, 0.0)
            parts = [jnp.zeros_like(block)] * heads
            parts[h] = block
            blocks.append(jnp.concatenate(parts, axis=1))
        if rows > heads * GROUP:
            blocks.append(jnp.zeros((rows - heads * GROUP, cols), jnp.float32))
        queries.append(jnp.concatenate(blocks, axis=0))

    scores, masks = [], []
    for r in range(num_req):
        length = lens_ref[r]
        query = queries[r].astype(pool_ref.dtype)
        score = jnp.concatenate(
            [
                lax.dot_general(
                    query, pool_ref[table_ref[r, p]], (((1,), (1,)), ((), ())),
                    preferred_element_type=jnp.float32,
                )
                for p in range(MAXP)
            ],
            axis=1,
        )
        own = jnp.sum(queries[r] * fresh[r : r + 1, :], axis=1, keepdims=True)
        positions = lax.broadcasted_iota(jnp.int32, score.shape, 1)
        score = jnp.where(positions == length, own, score) * (1.0 / math.sqrt(HD))
        scores.append(jnp.where(positions <= length, score, -jnp.inf))
        masks.append(positions == length)
    score = jnp.concatenate(scores, axis=0)
    mask = jnp.concatenate(masks, axis=0)
    weights = jnp.exp(score - jnp.max(score, axis=1, keepdims=True))
    probs = (weights / jnp.sum(weights, axis=1, keepdims=True)).astype(pool_ref.dtype).astype(jnp.float32)
    own = jnp.sum(jnp.where(mask, probs, 0.0), axis=1, keepdims=True)
    probs = jnp.where(mask, 0.0, probs).astype(pool_ref.dtype)

    attn = []
    for r in range(num_req):
        out = own[r * rows : (r + 1) * rows, :] * fresh[r : r + 1, :]
        for p in range(MAXP):
            out = out + jnp.dot(
                probs[r * rows : (r + 1) * rows, p * PAGE : (p + 1) * PAGE], pool_ref[table_ref[r, p]],
                preferred_element_type=jnp.float32,
            )
        attn.append(
            jnp.concatenate(
                [
                    out[i : i + 1, i // GROUP * LANES + HD : (i // GROUP + 1) * LANES]
                    for i in range(heads * GROUP)
                ],
                axis=1,
            )
        )
    attn = jnp.concatenate(attn, axis=0).astype(proj_ref.dtype)
    proj_read.wait()
    head_ref[...] = jnp.dot(attn, proj_ref[...], preferred_element_type=jnp.float32)
    for write in writes:
        write.wait()


def attend(leave_slot, page_table, req_lengths, qkv_new, kv_pool, out_proj):
    num_req = qkv_new.shape[0]
    cols = kv_pool.shape[2]
    return pl.pallas_call(
        attend_kernel,
        out_shape=(
            jax.ShapeDtypeStruct((num_req, out_proj.shape[1]), jnp.float32),
            jax.ShapeDtypeStruct((num_req, PAGE, cols), kv_pool.dtype),
            jax.ShapeDtypeStruct((1, LANES), jnp.float32),
        ),
        in_specs=[SMEM, SMEM, SMEM, VMEM, VMEM, HBM],
        out_specs=(VMEM, HBM, VMEM),
        scratch_shapes=[
            pltpu.VMEM((num_req, PAGE, cols), kv_pool.dtype),
            pltpu.VMEM(out_proj.shape, out_proj.dtype),
            pltpu.SemaphoreType.DMA((num_req,)),
            pltpu.SemaphoreType.DMA,
        ],
        compiler_params=params(),
        cost_estimate=pl.CostEstimate(
            flops=2 * num_req * (2 * 16 * SPAN * cols + out_proj.size),
            bytes_accessed=2 * (num_req * SPAN * cols + out_proj.size),
            transcendentals=num_req * 16 * SPAN,
        ),
        name="attend",
    )(leave_slot, page_table, req_lengths, qkv_new, kv_pool, in_hbm(out_proj))


def experts_kernel(
    index_ref, ids_ref, gates_ref, resid_ref, gain_ref, in_ref, down_ref, *parts_refs
):
    *parts_refs, stream_ref, total_ref = parts_refs
    head = parts_refs[0][...]
    for part in parts_refs[1:]:
        head = head + part[...]
    stream = resid_ref[...].astype(jnp.float32) + head
    stream_ref[...] = stream
    mean_sq = jnp.mean(stream * stream, axis=1, keepdims=True)
    normed = (stream * lax.rsqrt(mean_sq + 1e-05) * gain_ref[...]).astype(in_ref.dtype)
    both = jnp.dot(normed, in_ref[0], preferred_element_type=jnp.float32)
    gate = both[:, :FF]
    acted = (gate / (1.0 + jnp.exp(-gate)) * both[:, FF:]).astype(down_ref.dtype)
    chosen = ids_ref[...] == index_ref[0]
    route = jnp.sum(
        jnp.where(chosen, gates_ref[...].astype(jnp.float32), 0.0), axis=1, keepdims=True
    )
    total_ref[...] = route * jnp.dot(acted, down_ref[0], preferred_element_type=jnp.float32)


def experts(tp_index, expert_ids, gate_weights, resid, norm_gain, expert_in, expert_down, parts):
    shape = jax.ShapeDtypeStruct(resid.shape, jnp.float32)
    return pl.pallas_call(
        experts_kernel,
        out_shape=(shape, shape),
        in_specs=[SMEM] + [VMEM] * (6 + len(parts)),
        out_specs=(VMEM, VMEM),
        compiler_params=params(),
        cost_estimate=pl.CostEstimate(
            flops=2 * resid.shape[0] * (expert_in.size + expert_down.size),
            bytes_accessed=2 * (expert_in.size + expert_down.size),
            transcendentals=resid.shape[0] * FF,
        ),
        name="experts",
    )(
        tp_index, expert_ids, gate_weights, resid, norm_gain[None, :], expert_in, expert_down, *parts
    )


def forward_kernel(
    mesh_shape, leave_ref, target_ref, tp_ref, index_ref, landed_ref, hidden_ref, note_ref, taken_ref, send_ref
):
    pieces, rows, cols = landed_ref.shape
    body = rows * cols // LANES
    send_ref[:, body:, :] = jnp.zeros((pieces, EXTRA, LANES), send_ref.dtype)
    own = place_of(index_ref[0], tp_ref[0], SPREAD.get(mesh_shape, ()))
    lane = lax.broadcasted_iota(jnp.int32, (1, LANES), 1)
    for s in range(pieces):
        last = landed_ref[s, rows - 1 :, :LANES].astype(jnp.float32)
        place = jnp.max(jnp.where(lane == own, last, 0.0)).astype(jnp.int32)
        for c in range(cols // LANES):
            send_ref[place, c * rows : (c + 1) * rows, :] = landed_ref[s, :, c * LANES : (c + 1) * LANES]
    hidden = hidden_ref[...].astype(jnp.float32)
    at_row = lax.broadcasted_iota(jnp.int32, hidden.shape, 0) == leave_ref[0]
    row = jnp.sum(jnp.where(at_row, hidden, 0.0), axis=0, keepdims=True)
    spare = (EXTRA - 2) * LANES - row.shape[1]
    if spare:
        row = jnp.concatenate([row, jnp.zeros((1, spare), jnp.float32)], axis=1)
    lines = [row[:, k * LANES : (k + 1) * LANES] for k in range(EXTRA - 2)]
    place = place_of(target_ref[0], tp_ref[0], DELIVER.get(mesh_shape, ()))
    extra = jnp.concatenate(lines + [taken_ref[...], note_ref[...]], axis=0)
    send_ref[place, body:, :] = extra.astype(send_ref.dtype)


def forward(mesh_shape, leave_slot, target_rep, tp_index, rep_index, landed, hidden, note, taken):
    pieces, rows, cols = landed.shape
    return pl.pallas_call(
        functools.partial(forward_kernel, mesh_shape),
        out_shape=jax.ShapeDtypeStruct((pieces, rows * cols // LANES + EXTRA, LANES), landed.dtype),
        in_specs=[SMEM] * 4 + [VMEM] * 4,
        out_specs=VMEM,
        compiler_params=params(),
        name="forward",
    )(leave_slot, target_rep, tp_index, rep_index, landed, hidden, note, taken)


def settle_kernel(
    mesh_shape, leave_ref, tp_ref, landed_ref, hidden_ref, new_in_ref, hidden_out_ref, new_ref, arrived_ref,
    pages, mixed, page_sems, new_sem, hidden_sem,
):
    del new_in_ref
    pieces, slot_rows, _ = landed_ref.shape
    body = slot_rows - EXTRA
    cols = pages.shape[2]
    rows = SPAN // pieces
    leave = leave_ref[0]
    orders = list(zip(SPREAD.get(mesh_shape, ()), DELIVER.get(mesh_shape, ())))
    extra = jnp.sum(landed_ref[:, body:, :].astype(jnp.float32), axis=0)
    taken = extra[EXTRA - 2 : EXTRA - 1, :]
    row_in = lax.broadcasted_iota(jnp.int32, (rows, LANES), 0)
    lane = lax.broadcasted_iota(jnp.int32, (rows, LANES), 1)
    writes = []
    for p in range(MAXP):
        for j in range(p * pieces // MAXP, (p + 1) * pieces // MAXP):
            start = j * rows - p * PAGE
            slot = j
            for core, (spread, deliver) in enumerate(orders):
                slot = jnp.where(tp_ref[0] == core, deliver.index(spread[j]), slot)
            for c in range(cols // LANES):
                block = landed_ref[slot, c * rows : (c + 1) * rows, :]
                if c == 0:
                    at = jnp.logical_and(row_in == rows - 1, lane == j)
                    block = jnp.where(at, taken, block.astype(jnp.float32)).astype(pages.dtype)
                pages[p, start : start + rows, c * LANES : (c + 1) * LANES] = block
        writes.append(pltpu.make_async_copy(pages.at[p], arrived_ref.at[p], page_sems.at[p]))
        writes[p].start()
    page = jnp.max(extra[EXTRA - 1 :, :]).astype(jnp.int32)
    writes.append(pltpu.make_async_copy(pages.at[page], new_ref.at[leave], new_sem))
    writes[-1].start()
    width = hidden_ref.shape[1]
    row = jnp.concatenate([extra[k : k + 1, :] for k in range(-(-width // LANES))], axis=1)
    hidden = hidden_ref[...].astype(jnp.float32)
    at_row = lax.broadcasted_iota(jnp.int32, hidden.shape, 0) == leave
    mixed[...] = jnp.where(at_row, row[:, :width], hidden).astype(mixed.dtype)
    writes.append(pltpu.make_async_copy(mixed, hidden_out_ref, hidden_sem))
    writes[-1].start()
    for write in writes:
        write.wait()


def settle(mesh_shape, leave_slot, tp_index, landed, hidden, new_pages):
    arrived = (MAXP,) + new_pages.shape[1:]
    return pl.pallas_call(
        functools.partial(settle_kernel, mesh_shape),
        out_shape=(
            jax.ShapeDtypeStruct(hidden.shape, hidden.dtype),
            jax.ShapeDtypeStruct(new_pages.shape, new_pages.dtype),
            jax.ShapeDtypeStruct(arrived, new_pages.dtype),
        ),
        in_specs=[SMEM, SMEM, VMEM, VMEM, HBM],
        out_specs=(HBM, HBM, HBM),
        scratch_shapes=[
            pltpu.VMEM(arrived, new_pages.dtype),
            pltpu.VMEM(hidden.shape, hidden.dtype),
            pltpu.SemaphoreType.DMA((MAXP,)),
            pltpu.SemaphoreType.DMA,
            pltpu.SemaphoreType.DMA,
        ],
        input_output_aliases={4: 1},
        compiler_params=params(),
        name="settle",
    )(leave_slot, tp_index, landed, hidden, new_pages)


def local(
    kv_pool,
    page_table,
    req_lengths,
    leave_slot,
    target_rep,
    qkv_new,
    residual_in,
    expert_ids,
    gate_weights,
    norm_gain,
    out_proj,
    expert_in,
    expert_down,
):
    pieces, tp_size = mesh_shape = lax.axis_size("rep"), lax.axis_size("tp")
    rep_index, tp_index = lax.axis_index("rep")[None], lax.axis_index("tp")[None]

    def exchange(packet, orders):
        orders = orders.get(mesh_shape, (tuple(range(pieces)),) * tp_size)
        groups = [[peer * tp_size + core for peer in peers] for core, peers in enumerate(orders)]
        return lax.all_to_all(
            packet, ("rep", "tp"), split_axis=0, concat_axis=0, tiled=True, axis_index_groups=groups
        )

    send, taken = pack(
        mesh_shape, leave_slot, target_rep, tp_index, page_table, req_lengths, qkv_new, kv_pool
    )
    send, qkv_new, kv_pool = lax.optimization_barrier((send, qkv_new, kv_pool))
    landed = exchange(send.reshape(pieces, SPAN // pieces, kv_pool.shape[2]), SPREAD)

    head_part, new_pages, note = attend(
        leave_slot, page_table, req_lengths, qkv_new, kv_pool, out_proj
    )
    shifts = [[(i, (i + k) % tp_size) for i in range(tp_size)] for k in range(1, tp_size)]
    parts = [head_part] + [lax.ppermute(head_part, "tp", shift) for shift in shifts]
    assert expert_in.shape[0] == 1
    stream, total = experts(
        tp_index, expert_ids, gate_weights, residual_in, norm_gain, expert_in, expert_down, parts
    )
    width = stream.shape[1] // tp_size

    def share(values, index):
        return lax.dynamic_slice_in_dim(values, index * width, width, 1)

    mix = share(total, tp_index[0])
    for k, shift in enumerate(shifts, 1):
        mix = mix + lax.ppermute(share(total, (tp_index[0] + k) % tp_size), "tp", shift)
    hidden = (share(stream, tp_index[0]) + mix).astype(jnp.bfloat16)
    landed = exchange(
        forward(mesh_shape, leave_slot, target_rep, tp_index, rep_index, landed, hidden, note, taken),
        DELIVER,
    )
    return settle(mesh_shape, leave_slot, tp_index, landed, hidden, new_pages)


def solution(mesh):
    return jax.shard_map(
        local,
        mesh=mesh,
        in_specs=(
            P("rep", None, "tp"),
            P("rep", None),
            P("rep"),
            P("rep"),
            P("rep"),
            P("rep", "tp"),
            P("rep", None),
            P("rep", None),
            P("rep", None),
            P(),
            P("tp", None),
            P("tp", None, None),
            P("tp", None, None),
        ),
        out_specs=(P("rep", "tp"), P("rep", None, "tp"), P("rep", None, "tp")),
        check_vma=False,
    )
```

```python
import functools
import math

import jax
import jax.numpy as jnp
from jax import lax
from jax.experimental import pallas as pl
from jax.experimental.pallas import tpu as pltpu
from jax.sharding import PartitionSpec as P

QH = 24
KVH = 8
HD = 64
FF = 256
PAGE = 128
MAXP = 4
GROUP = QH // KVH
SPAN = MAXP * PAGE
LANES = 128
HALF = PAGE // 2
EXTRA = 8
VMEM_BYTES = 16 * 1024 * 1024
SPREAD = {(16, 2): (
    (0, 8, 2, 3, 4, 5, 6, 13, 1, 15, 10, 11, 14, 7, 12, 9),
    (10, 9, 8, 11, 4, 15, 12, 0, 2, 3, 1, 13, 14, 7, 6, 5),
)}
DELIVER = {(16, 2): (
    (3, 8, 2, 0, 4, 5, 6, 13, 1, 15, 10, 11, 14, 7, 12, 9),
    (10, 9, 12, 11, 4, 15, 8, 6, 2, 3, 5, 13, 14, 7, 0, 1),
)}

SMEM = pl.BlockSpec(memory_space=pltpu.SMEM)
VMEM = pl.BlockSpec(memory_space=pltpu.VMEM)
HBM = pl.BlockSpec(memory_space=pltpu.HBM)


def in_hbm(array):
    return pltpu.with_memory_space_constraint(array, pltpu.HBM)


def params():
    return pltpu.CompilerParams(vmem_limit_bytes=VMEM_BYTES)


def place_of(replica, tp_index, orders):
    place = replica
    for core, peers in enumerate(orders):
        for k, peer in enumerate(peers):
            hit = jnp.logical_and(replica == peer, tp_index == core)
            place = jnp.where(hit, k, place)
    return place


def fresh_of(qkv, cols):
    width = (GROUP + 2) * HD
    return jnp.concatenate(
        [qkv[:, h * width + GROUP * HD : (h + 1) * width] for h in range(cols // LANES)], axis=1
    )


def put_row(ref, lead, row, fresh):
    start = pl.multiple_of(row // 16 * 16, 16)
    block = ref[lead, pl.ds(start, 16), :].astype(jnp.float32)
    at_row = lax.broadcasted_iota(jnp.int32, block.shape, 0) == row - start
    ref[lead, pl.ds(start, 16), :] = jnp.where(at_row, fresh, block).astype(ref.dtype)


def pack_kernel(
    mesh_shape, leave_ref, target_ref, tp_ref, table_hbm, lens_hbm, qkv_hbm, pool_ref, send_ref, taken_ref,
    table_ref, lens_ref, qkv_ref, pages, small_sems, page_sems, send_sems,
):
    smalls = [
        pltpu.make_async_copy(source, target, small_sems.at[i])
        for i, (source, target) in enumerate(
            [(table_hbm, table_ref), (lens_hbm, lens_ref), (qkv_hbm, qkv_ref)]
        )
    ]
    for copy in smalls:
        copy.start()
    smalls[0].wait()
    leave = leave_ref[0]
    copies = [
        pltpu.make_async_copy(pool_ref.at[table_ref[leave, p]], pages.at[p], page_sems.at[p])
        for p in range(MAXP)
    ]
    for copy in copies:
        copy.start()
    cols = pages.shape[2]
    pieces = mesh_shape[0]
    rows = SPAN // pieces
    ticket = place_of(target_ref[0], tp_ref[0], DELIVER.get(mesh_shape, ())).astype(jnp.float32)
    smalls[1].wait()
    smalls[2].wait()
    qkv = qkv_ref[...].astype(jnp.float32)
    at_row = lax.broadcasted_iota(jnp.int32, qkv.shape, 0) == leave
    qkv = jnp.sum(jnp.where(at_row, qkv, 0.0), axis=0, keepdims=True)
    fresh = fresh_of(qkv, cols)
    length = lens_ref[leave]
    taken = jnp.zeros((16, LANES), jnp.float32)
    row_in = lax.broadcasted_iota(jnp.int32, taken.shape, 0)
    lane = lax.broadcasted_iota(jnp.int32, taken.shape, 1)
    sends = []
    for p in range(MAXP):
        copies[p].wait()

        @pl.when(length // PAGE == p)
        def _():
            put_row(pages, p, length % PAGE, fresh)

        for j in range(p * pieces // MAXP, (p + 1) * pieces // MAXP):
            last = (j + 1) * rows - 1 - p * PAGE
            start = last // 16 * 16
            block = pages[p, start : start + 16, :LANES].astype(jnp.float32)
            at = jnp.logical_and(row_in == last - start, lane == j)
            taken = taken + jnp.where(at, block, 0.0)
            pages[p, start : start + 16, :LANES] = jnp.where(at, ticket, block).astype(pages.dtype)
        sends.append(pltpu.make_async_copy(pages.at[p], send_ref.at[p], send_sems.at[p]))
        sends[p].start()
    taken_ref[...] = jnp.sum(taken, axis=0, keepdims=True)
    for send in sends:
        send.wait()


def pack(mesh_shape, leave_slot, target_rep, tp_index, page_table, req_lengths, qkv_new, kv_pool):
    cols = kv_pool.shape[2]
    pieces = mesh_shape[0]
    assert pieces % MAXP == 0 and pieces <= LANES
    return pl.pallas_call(
        functools.partial(pack_kernel, mesh_shape),
        out_shape=(
            pltpu.HBM((MAXP, PAGE, cols), kv_pool.dtype),
            jax.ShapeDtypeStruct((1, LANES), jnp.float32),
        ),
        in_specs=[SMEM] * 3 + [HBM] * 4,
        out_specs=(HBM, VMEM),
        scratch_shapes=[
            pltpu.SMEM(page_table.shape, page_table.dtype),
            pltpu.SMEM(req_lengths.shape, req_lengths.dtype),
            pltpu.VMEM(qkv_new.shape, qkv_new.dtype),
            pltpu.VMEM((MAXP, PAGE, cols), kv_pool.dtype),
            pltpu.SemaphoreType.DMA((3,)),
            pltpu.SemaphoreType.DMA((MAXP,)),
            pltpu.SemaphoreType.DMA((MAXP,)),
        ],
        compiler_params=params(),
        name="pack",
    )(leave_slot, target_rep, tp_index, *map(in_hbm, (page_table, req_lengths, qkv_new, kv_pool)))


def attend_kernel(
    leave_ref, table_ref, lens_ref, qkv_ref, pool_ref, proj_hbm, head_ref, new_ref, note_ref,
    stage, proj_ref, sems, proj_sem,
):
    proj_read = pltpu.make_async_copy(proj_hbm, proj_ref, proj_sem)
    proj_read.start()
    note = (lens_ref[leave_ref[0]] // PAGE).astype(jnp.float32)
    note_ref[...] = jnp.full(note_ref.shape, note, jnp.float32)
    num_req = qkv_ref.shape[0]
    cols = pool_ref.shape[2]
    heads = cols // LANES
    rows = -(-heads * GROUP // 16) * 16
    width = (GROUP + 2) * HD
    qkv = qkv_ref[...].astype(jnp.float32)
    fresh = fresh_of(qkv, cols)

    writes = []
    for r in range(num_req):
        length = lens_ref[r]
        stage[r] = pool_ref[table_ref[r, length // PAGE]]
        put_row(stage, r, length % PAGE, fresh[r : r + 1, :])
        write = pltpu.make_async_copy(stage.at[r], new_ref.at[r], sems.at[r])
        write.start()
        writes.append(write)

    queries = []
    for r in range(num_req):
        blocks = []
        for h in range(heads):
            block = jnp.concatenate(
                [qkv[r : r + 1, h * width + g * HD : h * width + (g + 2) * HD] for g in range(GROUP)], axis=0
            )
            lane = lax.broadcasted_iota(jnp.int32, block.shape, 1)
            block = jnp.where(lane < HD, block, 0.0)
            parts = [jnp.zeros_like(block)] * heads
            parts[h] = block
            blocks.append(jnp.concatenate(parts, axis=1))
        if rows > heads * GROUP:
            blocks.append(jnp.zeros((rows - heads * GROUP, cols), jnp.float32))
        queries.append(jnp.concatenate(blocks, axis=0))

    scores, masks = [], []
    for r in range(num_req):
        length = lens_ref[r]
        query = queries[r].astype(pool_ref.dtype)
        score = jnp.concatenate(
            [
                lax.dot_general(
                    query, pool_ref[table_ref[r, p]], (((1,), (1,)), ((), ())),
                    preferred_element_type=jnp.float32,
                )
                for p in range(MAXP)
            ],
            axis=1,
        )
        own = jnp.sum(queries[r] * fresh[r : r + 1, :], axis=1, keepdims=True)
        positions = lax.broadcasted_iota(jnp.int32, score.shape, 1)
        score = jnp.where(positions == length, own, score) * (1.0 / math.sqrt(HD))
        scores.append(jnp.where(positions <= length, score, -jnp.inf))
        masks.append(positions == length)
    score = jnp.concatenate(scores, axis=0)
    mask = jnp.concatenate(masks, axis=0)
    weights = jnp.exp(score - jnp.max(score, axis=1, keepdims=True))
    probs = (weights / jnp.sum(weights, axis=1, keepdims=True)).astype(pool_ref.dtype).astype(jnp.float32)
    own = jnp.sum(jnp.where(mask, probs, 0.0), axis=1, keepdims=True)
    probs = jnp.where(mask, 0.0, probs).astype(pool_ref.dtype)

    attn = []
    for r in range(num_req):
        out = own[r * rows : (r + 1) * rows, :] * fresh[r : r + 1, :]
        for p in range(MAXP):
            out = out + jnp.dot(
                probs[r * rows : (r + 1) * rows, p * PAGE : (p + 1) * PAGE], pool_ref[table_ref[r, p]],
                preferred_element_type=jnp.float32,
            )
        attn.append(
            jnp.concatenate(
                [
                    out[i : i + 1, i // GROUP * LANES + HD : (i // GROUP + 1) * LANES]
                    for i in range(heads * GROUP)
                ],
                axis=1,
            )
        )
    attn = jnp.concatenate(attn, axis=0).astype(proj_ref.dtype)
    proj_read.wait()
    head_ref[...] = jnp.dot(attn, proj_ref[...], preferred_element_type=jnp.float32)
    for write in writes:
        write.wait()


def attend(leave_slot, page_table, req_lengths, qkv_new, kv_pool, out_proj):
    num_req = qkv_new.shape[0]
    cols = kv_pool.shape[2]
    return pl.pallas_call(
        attend_kernel,
        out_shape=(
            jax.ShapeDtypeStruct((num_req, out_proj.shape[1]), jnp.float32),
            jax.ShapeDtypeStruct((num_req, PAGE, cols), kv_pool.dtype),
            jax.ShapeDtypeStruct((1, LANES), jnp.float32),
        ),
        in_specs=[SMEM, SMEM, SMEM, VMEM, VMEM, HBM],
        out_specs=(VMEM, HBM, VMEM),
        scratch_shapes=[
            pltpu.VMEM((num_req, PAGE, cols), kv_pool.dtype),
            pltpu.VMEM(out_proj.shape, out_proj.dtype),
            pltpu.SemaphoreType.DMA((num_req,)),
            pltpu.SemaphoreType.DMA,
        ],
        compiler_params=params(),
        cost_estimate=pl.CostEstimate(
            flops=2 * num_req * (2 * 16 * SPAN * cols + out_proj.size),
            bytes_accessed=2 * (num_req * SPAN * cols + out_proj.size),
            transcendentals=num_req * 16 * SPAN,
        ),
        name="attend",
    )(leave_slot, page_table, req_lengths, qkv_new, kv_pool, in_hbm(out_proj))


def experts_kernel(
    index_ref, ids_ref, gates_ref, resid_ref, gain_ref, in_ref, down_ref, *parts_refs
):
    *parts_refs, stream_ref, total_ref = parts_refs
    head = parts_refs[0][...]
    for part in parts_refs[1:]:
        head = head + part[...]
    stream = resid_ref[...].astype(jnp.float32) + head
    stream_ref[...] = stream
    mean_sq = jnp.mean(stream * stream, axis=1, keepdims=True)
    normed = (stream * lax.rsqrt(mean_sq + 1e-05) * gain_ref[...]).astype(in_ref.dtype)
    both = jnp.dot(normed, in_ref[0], preferred_element_type=jnp.float32)
    gate = both[:, :FF]
    acted = (gate / (1.0 + jnp.exp(-gate)) * both[:, FF:]).astype(down_ref.dtype)
    chosen = ids_ref[...] == index_ref[0]
    route = jnp.sum(
        jnp.where(chosen, gates_ref[...].astype(jnp.float32), 0.0), axis=1, keepdims=True
    )
    total_ref[...] = route * jnp.dot(acted, down_ref[0], preferred_element_type=jnp.float32)


def experts(tp_index, expert_ids, gate_weights, resid, norm_gain, expert_in, expert_down, parts):
    shape = jax.ShapeDtypeStruct(resid.shape, jnp.float32)
    return pl.pallas_call(
        experts_kernel,
        out_shape=(shape, shape),
        in_specs=[SMEM] + [VMEM] * (6 + len(parts)),
        out_specs=(VMEM, VMEM),
        compiler_params=params(),
        cost_estimate=pl.CostEstimate(
            flops=2 * resid.shape[0] * (expert_in.size + expert_down.size),
            bytes_accessed=2 * (expert_in.size + expert_down.size),
            transcendentals=resid.shape[0] * FF,
        ),
        name="experts",
    )(
        tp_index, expert_ids, gate_weights, resid, norm_gain[None, :], expert_in, expert_down, *parts
    )


def forward_kernel(
    mesh_shape, leave_ref, target_ref, tp_ref, index_ref, landed_ref, hidden_ref, note_ref, taken_ref, send_ref
):
    pieces, rows, cols = landed_ref.shape
    body = rows * cols // LANES
    send_ref[:, body:, :] = jnp.zeros((pieces, EXTRA, LANES), send_ref.dtype)
    own = place_of(index_ref[0], tp_ref[0], SPREAD.get(mesh_shape, ()))
    lane = lax.broadcasted_iota(jnp.int32, (1, LANES), 1)
    for s in range(pieces):
        last = landed_ref[s, rows - 1 :, :LANES].astype(jnp.float32)
        place = jnp.max(jnp.where(lane == own, last, 0.0)).astype(jnp.int32)
        for c in range(cols // LANES):
            send_ref[place, c * rows : (c + 1) * rows, :] = landed_ref[s, :, c * LANES : (c + 1) * LANES]
    hidden = hidden_ref[...].astype(jnp.float32)
    at_row = lax.broadcasted_iota(jnp.int32, hidden.shape, 0) == leave_ref[0]
    row = jnp.sum(jnp.where(at_row, hidden, 0.0), axis=0, keepdims=True)
    spare = (EXTRA - 2) * LANES - row.shape[1]
    if spare:
        row = jnp.concatenate([row, jnp.zeros((1, spare), jnp.float32)], axis=1)
    lines = [row[:, k * LANES : (k + 1) * LANES] for k in range(EXTRA - 2)]
    place = place_of(target_ref[0], tp_ref[0], DELIVER.get(mesh_shape, ()))
    extra = jnp.concatenate(lines + [taken_ref[...], note_ref[...]], axis=0)
    send_ref[place, body:, :] = extra.astype(send_ref.dtype)


def forward(mesh_shape, leave_slot, target_rep, tp_index, rep_index, landed, hidden, note, taken):
    pieces, rows, cols = landed.shape
    return pl.pallas_call(
        functools.partial(forward_kernel, mesh_shape),
        out_shape=jax.ShapeDtypeStruct((pieces, rows * cols // LANES + EXTRA, LANES), landed.dtype),
        in_specs=[SMEM] * 4 + [VMEM] * 4,
        out_specs=VMEM,
        compiler_params=params(),
        name="forward",
    )(leave_slot, target_rep, tp_index, rep_index, landed, hidden, note, taken)


def settle_kernel(
    mesh_shape, leave_ref, tp_ref, landed_ref, hidden_ref, new_in_ref, hidden_out_ref, new_ref, arrived_ref,
    pages, mixed, page_sems, new_sem, hidden_sem,
):
    del new_in_ref
    pieces, slot_rows, _ = landed_ref.shape
    body = slot_rows - EXTRA
    cols = pages.shape[2]
    rows = SPAN // pieces
    leave = leave_ref[0]
    orders = list(zip(SPREAD.get(mesh_shape, ()), DELIVER.get(mesh_shape, ())))
    extra = jnp.sum(landed_ref[:, body:, :].astype(jnp.float32), axis=0)
    taken = extra[EXTRA - 2 : EXTRA - 1, :]
    row_in = lax.broadcasted_iota(jnp.int32, (rows, LANES), 0)
    lane = lax.broadcasted_iota(jnp.int32, (rows, LANES), 1)
    writes = []
    for p in range(MAXP):
        for j in range(p * pieces // MAXP, (p + 1) * pieces // MAXP):
            start = j * rows - p * PAGE
            slot = j
            for core, (spread, deliver) in enumerate(orders):
                slot = jnp.where(tp_ref[0] == core, deliver.index(spread[j]), slot)
            for c in range(cols // LANES):
                block = landed_ref[slot, c * rows : (c + 1) * rows, :]
                if c == 0:
                    at = jnp.logical_and(row_in == rows - 1, lane == j)
                    block = jnp.where(at, taken, block.astype(jnp.float32)).astype(pages.dtype)
                pages[p, start : start + rows, c * LANES : (c + 1) * LANES] = block
            if (start + rows) % HALF == 0:
                span = pl.ds(start + rows - HALF, HALF)
                writes.append(
                    pltpu.make_async_copy(
                        pages.at[p, span], arrived_ref.at[p, span], page_sems.at[len(writes)]
                    )
                )
                writes[-1].start()
    page = jnp.max(extra[EXTRA - 1 :, :]).astype(jnp.int32)
    writes.append(pltpu.make_async_copy(pages.at[page], new_ref.at[leave], new_sem))
    writes[-1].start()
    width = hidden_ref.shape[1]
    row = jnp.concatenate([extra[k : k + 1, :] for k in range(-(-width // LANES))], axis=1)
    hidden = hidden_ref[...].astype(jnp.float32)
    at_row = lax.broadcasted_iota(jnp.int32, hidden.shape, 0) == leave
    mixed[...] = jnp.where(at_row, row[:, :width], hidden).astype(mixed.dtype)
    writes.append(pltpu.make_async_copy(mixed, hidden_out_ref, hidden_sem))
    writes[-1].start()
    for write in writes:
        write.wait()


def settle(mesh_shape, leave_slot, tp_index, landed, hidden, new_pages):
    arrived = (MAXP,) + new_pages.shape[1:]
    return pl.pallas_call(
        functools.partial(settle_kernel, mesh_shape),
        out_shape=(
            jax.ShapeDtypeStruct(hidden.shape, hidden.dtype),
            jax.ShapeDtypeStruct(new_pages.shape, new_pages.dtype),
            jax.ShapeDtypeStruct(arrived, new_pages.dtype),
        ),
        in_specs=[SMEM, SMEM, VMEM, VMEM, HBM],
        out_specs=(HBM, HBM, HBM),
        scratch_shapes=[
            pltpu.VMEM(arrived, new_pages.dtype),
            pltpu.VMEM(hidden.shape, hidden.dtype),
            pltpu.SemaphoreType.DMA((SPAN // HALF,)),
            pltpu.SemaphoreType.DMA,
            pltpu.SemaphoreType.DMA,
        ],
        input_output_aliases={4: 1},
        compiler_params=params(),
        name="settle",
    )(leave_slot, tp_index, landed, hidden, new_pages)


def local(
    kv_pool,
    page_table,
    req_lengths,
    leave_slot,
    target_rep,
    qkv_new,
    residual_in,
    expert_ids,
    gate_weights,
    norm_gain,
    out_proj,
    expert_in,
    expert_down,
):
    pieces, tp_size = mesh_shape = lax.axis_size("rep"), lax.axis_size("tp")
    rep_index, tp_index = lax.axis_index("rep")[None], lax.axis_index("tp")[None]

    def exchange(packet, orders):
        orders = orders.get(mesh_shape, (tuple(range(pieces)),) * tp_size)
        groups = [[peer * tp_size + core for peer in peers] for core, peers in enumerate(orders)]
        return lax.all_to_all(
            packet, ("rep", "tp"), split_axis=0, concat_axis=0, tiled=True, axis_index_groups=groups
        )

    send, taken = pack(
        mesh_shape, leave_slot, target_rep, tp_index, page_table, req_lengths, qkv_new, kv_pool
    )
    send, qkv_new, kv_pool = lax.optimization_barrier((send, qkv_new, kv_pool))
    landed = exchange(send.reshape(pieces, SPAN // pieces, kv_pool.shape[2]), SPREAD)

    head_part, new_pages, note = attend(
        leave_slot, page_table, req_lengths, qkv_new, kv_pool, out_proj
    )
    shifts = [[(i, (i + k) % tp_size) for i in range(tp_size)] for k in range(1, tp_size)]
    parts = [head_part] + [lax.ppermute(head_part, "tp", shift) for shift in shifts]
    assert expert_in.shape[0] == 1
    stream, total = experts(
        tp_index, expert_ids, gate_weights, residual_in, norm_gain, expert_in, expert_down, parts
    )
    width = stream.shape[1] // tp_size

    def share(values, index):
        return lax.dynamic_slice_in_dim(values, index * width, width, 1)

    mix = share(total, tp_index[0])
    for k, shift in enumerate(shifts, 1):
        mix = mix + lax.ppermute(share(total, (tp_index[0] + k) % tp_size), "tp", shift)
    hidden = (share(stream, tp_index[0]) + mix).astype(jnp.bfloat16)
    landed = exchange(
        forward(mesh_shape, leave_slot, target_rep, tp_index, rep_index, landed, hidden, note, taken),
        DELIVER,
    )
    return settle(mesh_shape, leave_slot, tp_index, landed, hidden, new_pages)


def solution(mesh):
    return jax.shard_map(
        local,
        mesh=mesh,
        in_specs=(
            P("rep", None, "tp"),
            P("rep", None),
            P("rep"),
            P("rep"),
            P("rep"),
            P("rep", "tp"),
            P("rep", None),
            P("rep", None),
            P("rep", None),
            P(),
            P("tp", None),
            P("tp", None, None),
            P("tp", None, None),
        ),
        out_specs=(P("rep", "tp"), P("rep", None, "tp"), P("rep", None, "tp")),
        check_vma=False,
    )
```
